256 devices in a mesh: batch: 64 (over x, z, core), proto: 4 (over y).
Axes of the slice: x: 4, y: 4, z: 8, core: 2. Of those that a mesh axis runs over, the one named last changes fastest.
Arguments:
- teacher_tokens: bfloat16 [512, 256, 256], P('batch'), may hold values from -36 to 36
- student_tokens: bfloat16 [512, 256, 256], P('batch'), may hold values from -36 to 36
- masked_index: int32 [512, 64], P('batch'), may hold values from 0 to 255, as said below
- prototypes: bfloat16 [32768, 256], P(('batch', 'proto')), may hold values from -0.375 to 0.375
Outputs:
- loss: float32 [], replicated
- grad_student: bfloat16 [32768, 256], P('batch')
- grad_weight: float32 [32768, 256], P(('batch', 'proto'))
The draws below stay inside these ranges and needn't reach their ends.
Inputs may be any that keep to these rules, and one draw needn't show every extreme that they name: `masked_index`: each row holds 64 distinct patch positions of its image.
All inputs are finite; a program needn't handle non-finite values.
Results may differ from the reference program's by a relative error of at most 0.0049.
Values may be sent and summed in bfloat16 or wider, within the bound.
No kernel may reach another device: no remote copies, remote signals or barrier semaphores. Data moves between devices by JAX's collectives and lax.ppermute only.
A program may use at most 128 MiB of HBM per device.

```python
import math
import jax
import jax.numpy as jnp
from jax import lax

D = 256
PROTOS = 32768
PATCH = 256
MASKED = 64
ITERS = 3
IMAGES = 512


def token_draw(key, heavy):
    values = jnp.clip(jax.random.normal(key, (IMAGES, PATCH, D), jnp.float32), -6.0, 6.0)
    picks = jax.random.uniform(jax.random.fold_in(key, 7), (IMAGES, PATCH, 1)) < 0.04
    return values * jnp.where(picks, heavy, 1.0)


def draw_teacher_tokens(key, part):
    key = jax.random.fold_in(key, 1)
    return token_draw(key, 1.0).astype(jnp.bfloat16)


def draw_student_tokens(key, part):
    key = jax.random.fold_in(key, 2)
    return token_draw(key, 1.0).astype(jnp.bfloat16)


def draw_masked_index(key, part):
    key = jax.random.fold_in(key, 3)
    keys = jax.random.split(key, IMAGES)
    orders = jax.vmap(lambda single: jax.random.permutation(single, PATCH))(keys)
    return orders[:, :MASKED].astype(jnp.int32)


def block_scale(stream_key, shape, cuts, smallest, top_value):
    factor_of = 1.0
    for axis_at, shards_of in cuts:
        steps = jax.random.uniform(jax.random.fold_in(jax.random.fold_in(stream_key, 6), axis_at), (shards_of,), jnp.float32, smallest / len(cuts), top_value / len(cuts))
        factor_of = factor_of * jnp.repeat(jnp.exp(steps), shape[axis_at] // shards_of).reshape((-1,) + (1,) * (len(shape) - 1 - axis_at))
    return factor_of


def normal_values(key, extent, width, most, cuts=(), dtype=jnp.bfloat16):
    result = width * jax.random.normal(key, extent, jnp.float32)
    if cuts:
        result = result * block_scale(key, extent, cuts, -0.22, 0.18)
    return jnp.clip(result, -most, most).astype(dtype)


def setup_inputs(seed: int = 0) -> dict:
    streams_of = jax.random.split(jax.random.key(seed), 5)
    teacher_tokens = draw_teacher_tokens(jax.random.fold_in(streams_of[4], 71), 0)
    student_tokens = draw_student_tokens(jax.random.fold_in(streams_of[4], 71), 0)
    masked_index = draw_masked_index(jax.random.fold_in(streams_of[4], 71), 0)
    prototypes = normal_values(streams_of[3], (PROTOS, D), D ** -0.5, 0.375, ((0, 256),))
    return {"teacher_tokens": teacher_tokens, "student_tokens": student_tokens, "masked_index": masked_index, "prototypes": prototypes}


def reference(teacher_tokens, student_tokens, masked_index, prototypes):
    index = masked_index[:, :, None]
    teacher_rows = jnp.take_along_axis(teacher_tokens, index, axis=1).reshape(-1, D)
    student_rows = jnp.take_along_axis(student_tokens, index, axis=1).reshape(-1, D)
    total_rows = teacher_rows.shape[0]
    block = math.gcd(total_rows, 1024)
    teacher_blocks = teacher_rows.reshape(-1, block, D)
    student_blocks = student_rows.reshape(-1, block, D)

    def kernel(rows):
        scores = jnp.dot(rows, prototypes.T, preferred_element_type=jnp.float32) * (1.0 / 0.07)
        return jnp.exp(scores - jnp.max(scores, axis=1, keepdims=True))

    def first(carry, rows):
        return carry + jnp.sum(kernel(rows), axis=0), None

    colsum, _ = lax.scan(first, jnp.zeros((PROTOS,), jnp.float32), teacher_blocks)
    col_scale = 1.0 / colsum
    for step in range(ITERS - 1):
        def sweep(carry, rows, col_scale=col_scale):
            kern = kernel(rows)
            row_scale = 1.0 / jnp.sum(kern * col_scale[None, :], axis=1)
            return carry + jnp.sum(kern * row_scale[:, None], axis=0), None
        colsum, _ = lax.scan(sweep, jnp.zeros((PROTOS,), jnp.float32), teacher_blocks)
        col_scale = 1.0 / colsum

    def final(carry, pair):
        loss_acc, weight_acc = carry
        rows, srows = pair
        kern = kernel(rows)
        row_scale = 1.0 / jnp.sum(kern * col_scale[None, :], axis=1)
        targets = row_scale[:, None] * kern * col_scale[None, :]
        scores = jnp.dot(srows, prototypes.T, preferred_element_type=jnp.float32) * (1.0 / 0.1)
        top = jnp.max(scores, axis=1, keepdims=True)
        log_probs = scores - top - jnp.log(jnp.sum(jnp.exp(scores - top), axis=1, keepdims=True))
        loss_acc = loss_acc - jnp.sum(targets * log_probs)
        grad_logits = ((jnp.exp(log_probs) - targets) / (0.1 * total_rows)).astype(jnp.bfloat16)
        feature_grad = jnp.dot(grad_logits, prototypes, preferred_element_type=jnp.float32).astype(jnp.bfloat16)
        weight_acc = weight_acc + lax.dot_general(grad_logits, srows, (((0,), (0,)), ((), ())), preferred_element_type=jnp.float32)
        return (loss_acc, weight_acc), feature_grad

    init = (jnp.zeros((), jnp.float32), jnp.zeros((PROTOS, D), jnp.float32))
    (loss_acc, grad_weight), feature_blocks = lax.scan(final, init, (teacher_blocks, student_blocks))
    loss = loss_acc / total_rows
    return loss, feature_blocks.reshape(-1, D), grad_weight
```

```python
import functools

import jax
import jax.numpy as jnp
from jax import lax
from jax.experimental import pallas as pl
from jax.experimental.pallas import tpu as pltpu
from jax.sharding import Mesh, PartitionSpec as P

X, Z, C, Y = 4, 8, 2, 4
F32, BF16 = jnp.float32, jnp.bfloat16
D = 256
IMAGES = 8
MASKED = 64
OWN_ROWS = 512
OWN_PROTOS = 128
ROWS = X * OWN_ROWS
PROTOS = Z * C * OWN_PROTOS
TOTAL_ROWS = ROWS * Z * C
PEERS = X * Y
LANES = 128
GROUPS = 16
BLOCK = 256
HALVES = BLOCK // LANES
T_SCALE = 1.0 / 0.07
S_SCALE = 1.0 / 0.1
MIB = 1 << 20
TRANS_B = (((1,), (1,)), ((), ()))


def whole(shape):
    return pl.BlockSpec(shape, lambda *_: (0,) * len(shape))


def params(mib=32):
    return pltpu.CompilerParams(vmem_limit_bytes=mib * MIB, dimension_semantics=("arbitrary",))


def down(row):
    return jnp.transpose(jnp.broadcast_to(row, (LANES, LANES)))


def along(column_parts):
    return jnp.sum(jnp.transpose(column_parts), axis=0, keepdims=True)


def spread(ref, first, at, row):
    ref[:, pl.ds(first + at, 1), :] = jnp.broadcast_to(row[None], (ref.shape[0], 1, LANES))


def pick_kernel(index_ref, tokens_ref, out_ref):
    for image in range(IMAGES):
        at = lax.broadcasted_iota(jnp.int32, (D, MASKED), 0)
        chosen = (at == index_ref[image : image + 1, :]).astype(BF16)
        rows = lax.dot_general(
            chosen, tokens_ref[image], (((0,), (0,)), ((), ())), preferred_element_type=F32
        )
        out_ref[image * MASKED : (image + 1) * MASKED, :] = rows.astype(BF16)


def pick_rows(index, tokens):
    return pl.pallas_call(
        pick_kernel,
        out_shape=jax.ShapeDtypeStruct((OWN_ROWS, D), BF16),
        in_specs=[whole(index.shape), whole(tokens.shape)],
        out_specs=whole((OWN_ROWS, D)),
        grid=(1,),
        compiler_params=params(),
        name="pick_rows",
    )(index, tokens)


def place(pos_ref, pieces, out_ref, first=0, valid_ref=None):
    for number, piece in enumerate(pieces):
        size = piece.shape[0]
        at = pl.multiple_of(pos_ref[first + number] * size, size)
        if valid_ref is None:
            out_ref[pl.ds(at, size), :] = piece[...]
        else:
            @pl.when(valid_ref[number] == 1)
            def _(piece=piece, at=at, size=size):
                out_ref[pl.ds(at, size), :] = piece[...]


def teacher_kernel(xpos, wpos, wvalid, *refs):
    rows_in, protos_in = refs[:X], refs[X : X + 9]
    kern_ref, top_ref, tops_ref, protos_ref, rows_ref = refs[X + 9 :]
    step = pl.program_id(0)

    @pl.when(step == 0)
    def _():
        place(xpos, rows_in, rows_ref)
        place(wpos, protos_in, protos_ref, valid_ref=wvalid)

    rows = rows_ref[pl.ds(pl.multiple_of(step * BLOCK, BLOCK), BLOCK), :]
    scores = lax.dot_general(rows, protos_ref[...], TRANS_B, preferred_element_type=F32) * T_SCALE
    top = jnp.max(scores, axis=1, keepdims=True)
    kern_ref[...] = jnp.exp(scores - top).astype(BF16)
    for half in range(HALVES):
        part = jnp.broadcast_to(top[half * LANES : (half + 1) * LANES], (LANES, LANES))
        row = jnp.transpose(part)[0:1, :]
        top_ref[pl.ds(step * HALVES + half, 1), :] = row
        spread(tops_ref, 0, step * HALVES + half, row)


def teacher_scores(xpos, wpos, wvalid, rows, protos):
    return pl.pallas_call(
        teacher_kernel,
        out_shape=(
            jax.ShapeDtypeStruct((ROWS, PROTOS), BF16),
            jax.ShapeDtypeStruct((GROUPS, LANES), F32),
            jax.ShapeDtypeStruct((PEERS, GROUPS, LANES), F32),
            jax.ShapeDtypeStruct((PROTOS, D), BF16),
        ),
        grid_spec=pltpu.PrefetchScalarGridSpec(
            num_scalar_prefetch=3,
            grid=(ROWS // BLOCK,),
            in_specs=[whole(a.shape) for a in rows + protos],
            out_specs=(
                pl.BlockSpec((BLOCK, PROTOS), lambda i, *_: (i, 0)),
                whole((GROUPS, LANES)),
                whole((PEERS, GROUPS, LANES)),
                whole((PROTOS, D)),
            ),
            scratch_shapes=[pltpu.VMEM((ROWS, D), BF16)],
        ),
        compiler_params=params(),
        name="teacher_scores",
    )(xpos, wpos, wvalid, *rows, *protos)


def student_kernel(xpos, *refs):
    rows_in, protos_ref = refs[:X], refs[X]
    rows_ref, lse_ref = refs[X + 1 :]
    step = pl.program_id(0)

    @pl.when(step == 0)
    def _():
        place(xpos, rows_in, rows_ref)

    rows = rows_ref[pl.ds(pl.multiple_of(step * BLOCK, BLOCK), BLOCK), :]
    scores = lax.dot_general(rows, protos_ref[...], TRANS_B, preferred_element_type=F32) * S_SCALE
    top = jnp.max(scores, axis=1, keepdims=True)
    lse = top + jnp.log(jnp.sum(jnp.exp(scores - top), axis=1, keepdims=True))
    for half in range(HALVES):
        part = jnp.broadcast_to(lse[half * LANES : (half + 1) * LANES], (LANES, LANES))
        lse_ref[pl.ds(step * HALVES + half, 1), :] = jnp.transpose(part)[0:1, :]


def student_totals(xpos, rows, protos):
    return pl.pallas_call(
        student_kernel,
        out_shape=(
            jax.ShapeDtypeStruct((ROWS, D), BF16),
            jax.ShapeDtypeStruct((GROUPS, LANES), F32),
        ),
        grid_spec=pltpu.PrefetchScalarGridSpec(
            num_scalar_prefetch=1,
            grid=(ROWS // BLOCK,),
            in_specs=[whole(a.shape) for a in rows] + [whole((PROTOS, D))],
            out_specs=(whole((ROWS, D)), whole((GROUPS, LANES))),
        ),
        compiler_params=params(),
        name="student_totals",
    )(xpos, *rows, protos)


def row_weight(first, weight_ref, got_ref, top_ref, out_ref):
    if first:
        got = got_ref[0]
        for peer in range(1, PEERS):
            got = jnp.maximum(got, got_ref[peer])
        out_ref[...] = jnp.exp(top_ref[...] - got)
    else:
        out_ref[...] = weight_ref[...] / jnp.sum(got_ref[:, :GROUPS, :], axis=0)


def column_kernel(first, own_ref, got_ref, kern_ref, sums_ref, weight_ref, acc_ref):
    step = pl.program_id(0)

    @pl.when(step == 0)
    def _():
        row_weight(first, own_ref, got_ref, own_ref, weight_ref)
        acc_ref[...] = jnp.zeros_like(acc_ref)

    for half in range(HALVES):
        weight = down(weight_ref[pl.ds(step * HALVES + half, 1), :])
        for group in range(GROUPS):
            part = kern_ref[half * LANES : (half + 1) * LANES, group * LANES : (group + 1) * LANES]
            part = (part.astype(F32) * weight).reshape(LANES // 8, 8, LANES)
            acc_ref[group] += jnp.sum(part, axis=0)

    @pl.when(step == pl.num_programs(0) - 1)
    def _():
        for group in range(GROUPS):
            sums_ref[group : group + 1, :] = jnp.sum(acc_ref[group], axis=0, keepdims=True)


def column_pass(first, own, got, kern):
    return pl.pallas_call(
        functools.partial(column_kernel, first),
        out_shape=(
            jax.ShapeDtypeStruct((GROUPS, LANES), F32),
            jax.ShapeDtypeStruct((GROUPS, LANES), F32),
        ),
        grid=(ROWS // BLOCK,),
        in_specs=[
            whole(own.shape),
            whole(got.shape),
            pl.BlockSpec((BLOCK, PROTOS), lambda i: (i, 0)),
        ],
        out_specs=(whole((GROUPS, LANES)), whole((GROUPS, LANES))),
        scratch_shapes=[pltpu.VMEM((GROUPS, 8, LANES), F32)],
        compiler_params=params(),
        name="column_pass",
    )(own, got, kern)


def row_kernel(mode, weight_ref, mine_ref, theirs_ref, *refs):
    if mode == "lse":
        lse_ref, kern_ref, sums_ref, scale_ref = refs
    elif mode == "loss":
        rows_ref, protos_ref, kern_ref, sums_ref, scale_ref, scores_ref = refs
    else:
        kern_ref, sums_ref, scale_ref = refs
    step = pl.program_id(0)

    @pl.when(step == 0)
    def _():
        scale_ref[...] = 1.0 / (mine_ref[...] + theirs_ref[...])
        if mode == "lse":
            for group in range(GROUPS):
                spread(sums_ref, GROUPS, group, lse_ref[group : group + 1, :])

    if mode == "loss":
        scores_ref[...] = lax.dot_general(
            rows_ref[...], protos_ref[...], TRANS_B, preferred_element_type=F32
        )
    for half in range(HALVES):
        weight = down(weight_ref[pl.ds(step * HALVES + half, 1), :])
        total = jnp.zeros((LANES, LANES), F32)
        crossed = jnp.zeros((LANES, LANES), F32)
        for group in range(GROUPS):
            at = (slice(half * LANES, (half + 1) * LANES), slice(group * LANES, (group + 1) * LANES))
            part = (kern_ref[at].astype(F32) * weight) * scale_ref[group : group + 1, :]
            total += part
            if mode == "loss":
                crossed += part * scores_ref[at]
        spread(sums_ref, 0, step * HALVES + half, along(total))
        if mode == "loss":
            spread(sums_ref, GROUPS, step * HALVES + half, along(crossed) * S_SCALE)


def row_pass(mode, weight, mine, theirs, kern, extra=()):
    vectors = 1 if mode == "plain" else 2
    extra_specs, scratch = [], []
    if mode == "lse":
        extra_specs = [whole((GROUPS, LANES))]
    elif mode == "loss":
        extra_specs = [pl.BlockSpec((BLOCK, D), lambda i: (i, 0)), whole((PROTOS, D))]
        scratch = [pltpu.VMEM((BLOCK, PROTOS), F32)]
    return pl.pallas_call(
        functools.partial(row_kernel, mode),
        out_shape=(
            jax.ShapeDtypeStruct((PEERS, vectors * GROUPS, LANES), F32),
            jax.ShapeDtypeStruct((GROUPS, LANES), F32),
        ),
        grid=(ROWS // BLOCK,),
        in_specs=[whole((GROUPS, LANES))] * 3
        + extra_specs
        + [pl.BlockSpec((BLOCK, PROTOS), lambda i: (i, 0))],
        out_specs=(whole((PEERS, vectors * GROUPS, LANES)), whole((GROUPS, LANES))),
        scratch_shapes=scratch,
        compiler_params=params(),
        name="row_pass",
    )(weight, mine, theirs, *extra, kern)


def grad_kernel(
    core, weight_ref, got_ref, lses_ref, scale_ref, kern_ref, rows_ref, protos_ref,
    student_ref, keep_ref, send_ref, loss_ref, scaled_ref, lse_ref, scores_ref, logits_ref, acc_ref,
):
    step = pl.program_id(0)

    @pl.when(step == 0)
    def _():
        sums = jnp.sum(got_ref[:, :GROUPS, :], axis=0)
        crossed = jnp.sum(got_ref[:, GROUPS:, :], axis=0)
        top = lses_ref[0]
        for peer in range(1, PEERS):
            top = jnp.maximum(top, lses_ref[peer])
        total = jnp.zeros_like(top)
        for peer in range(PEERS):
            total += jnp.exp(lses_ref[peer] - top)
        lse = top + jnp.log(total)
        lse_ref[...] = lse
        scaled_ref[...] = weight_ref[...] / sums
        terms = (lse * sums - crossed) / sums
        terms = jnp.sum(jnp.sum(terms, axis=0, keepdims=True), axis=1, keepdims=True)
        loss_ref[...] = jnp.broadcast_to(terms, (8, LANES))
        acc_ref[...] = jnp.zeros_like(acc_ref)

    rows = rows_ref[...]
    scores_ref[...] = lax.dot_general(rows, protos_ref[...], TRANS_B, preferred_element_type=F32)
    for half in range(HALVES):
        weight = down(scaled_ref[pl.ds(step * HALVES + half, 1), :])
        lse = down(lse_ref[pl.ds(step * HALVES + half, 1), :])
        for group in range(GROUPS):
            at = (slice(half * LANES, (half + 1) * LANES), slice(group * LANES, (group + 1) * LANES))
            target = (kern_ref[at].astype(F32) * weight) * scale_ref[group : group + 1, :]
            prob = jnp.exp(scores_ref[at] * S_SCALE - lse)
            logits_ref[at] = ((prob - target) * (1.0 / (0.1 * TOTAL_ROWS))).astype(BF16)
    logits = logits_ref[...]
    student_ref[...] = jnp.dot(logits, protos_ref[...], preferred_element_type=F32).astype(BF16)
    acc_ref[...] += jnp.dot(jnp.transpose(rows), logits, preferred_element_type=F32)

    @pl.when(step == pl.num_programs(0) - 1)
    def _():
        for z in range(Z):
            for c in range(C):
                first = (z * C + c) * OWN_PROTOS
                part = jnp.transpose(acc_ref[:, first : first + OWN_PROTOS])

                @pl.when(core[0] == c)
                def _(part=part, z=z):
                    keep_ref[z] = part

                @pl.when(core[0] != c)
                def _(part=part, z=z):
                    send_ref[z] = part.astype(BF16)


def gradients(core, weight, got, lses, scale, kern, rows, protos):
    return pl.pallas_call(
        grad_kernel,
        out_shape=(
            jax.ShapeDtypeStruct((ROWS, D), BF16),
            jax.ShapeDtypeStruct((Z, OWN_PROTOS, D), F32),
            jax.ShapeDtypeStruct((Z, OWN_PROTOS, D), BF16),
            jax.ShapeDtypeStruct((8, LANES), F32),
        ),
        grid_spec=pltpu.PrefetchScalarGridSpec(
            num_scalar_prefetch=1,
            grid=(ROWS // BLOCK,),
            in_specs=[
                whole(weight.shape),
                whole(got.shape),
                whole(lses.shape),
                whole(scale.shape),
                pl.BlockSpec((BLOCK, PROTOS), lambda i, *_: (i, 0)),
                pl.BlockSpec((BLOCK, D), lambda i, *_: (i, 0)),
                whole((PROTOS, D)),
            ],
            out_specs=(
                pl.BlockSpec((BLOCK, D), lambda i, *_: (i, 0)),
                whole((Z, OWN_PROTOS, D)),
                whole((Z, OWN_PROTOS, D)),
                whole((8, LANES)),
            ),
            scratch_shapes=[
                pltpu.VMEM((GROUPS, LANES), F32),
                pltpu.VMEM((GROUPS, LANES), F32),
                pltpu.VMEM((BLOCK, PROTOS), F32),
                pltpu.VMEM((BLOCK, PROTOS), BF16),
                pltpu.VMEM((D, PROTOS), F32),
            ],
        ),
        compiler_params=params(),
        name="gradients",
    )(core, weight, got, lses, scale, kern, rows, protos)


TAIL = 16


def split_kernel(zs, keep_ref, got_ref, loss_ref, other_ref, mine_ref, *outs):
    step = pl.program_id(0)
    part = keep_ref[0] + got_ref[0].astype(F32)
    value = jnp.broadcast_to((loss_ref[...] + other_ref[...])[0:1, :], (TAIL, LANES))
    high = value.astype(BF16)
    rest = value - high.astype(F32)
    middle = rest.astype(BF16)
    low = (rest - middle.astype(F32)).astype(BF16)
    row = lax.broadcasted_iota(jnp.int32, (TAIL, LANES), 0)
    tail = jnp.where(row == 0, high.astype(F32), jnp.where(row == 1, middle.astype(F32), low.astype(F32)))
    tail = jnp.concatenate([tail, tail], axis=1).astype(BF16)
    for shift in range(Z):
        @pl.when(step == shift)
        def _(shift=shift):
            if shift == 0:
                mine_ref[...] = part
            else:
                outs[shift][:OWN_PROTOS, :] = part.astype(BF16)
            outs[shift][OWN_PROTOS:, :] = tail


def split_sums(zs, keep, got, loss, other):
    return pl.pallas_call(
        split_kernel,
        out_shape=(jax.ShapeDtypeStruct((OWN_PROTOS, D), F32),)
        + (jax.ShapeDtypeStruct((OWN_PROTOS + TAIL, D), BF16),) * Z,
        grid_spec=pltpu.PrefetchScalarGridSpec(
            num_scalar_prefetch=1,
            grid=(Z,),
            in_specs=[
                pl.BlockSpec((1, OWN_PROTOS, D), lambda i, zs: (zs[i], 0, 0)),
                pl.BlockSpec((1, OWN_PROTOS, D), lambda i, zs: (zs[i], 0, 0)),
                whole((8, LANES)),
                whole((8, LANES)),
            ],
            out_specs=(whole((OWN_PROTOS, D)),) + (whole((OWN_PROTOS + TAIL, D)),) * Z,
        ),
        compiler_params=params(),
        name="split_sums",
    )(zs, keep, got, loss, other)


def join_kernel(zfrom, mine_ref, *refs):
    parts, (out_ref, loss_ref, value_ref) = refs[:Z], refs[Z:]
    total = mine_ref[...]
    for shift, part in enumerate(parts):
        if shift:
            total += part[:OWN_PROTOS, :].astype(F32)
        tail = part[OWN_PROTOS:, :LANES].astype(F32)
        value_ref[pl.ds(zfrom[shift], 1), :] = tail[0:1] + (tail[1:2] + tail[2:3])
    out_ref[...] = total
    loss = value_ref[0:1, :]
    for z in range(1, Z):
        loss = loss + value_ref[z : z + 1, :]
    loss_ref[...] = jnp.broadcast_to(loss, (8, LANES)) * (1.0 / TOTAL_ROWS)


def join_sums(zfrom, mine, parts):
    return pl.pallas_call(
        join_kernel,
        out_shape=(jax.ShapeDtypeStruct((OWN_PROTOS, D), F32), jax.ShapeDtypeStruct((8, LANES), F32)),
        grid_spec=pltpu.PrefetchScalarGridSpec(
            num_scalar_prefetch=1,
            grid=(1,),
            in_specs=[whole(mine.shape)] + [whole(p.shape) for p in parts],
            out_specs=(whole((OWN_PROTOS, D)), whole((8, LANES))),
            scratch_shapes=[pltpu.VMEM((Z, LANES), F32)],
        ),
        compiler_params=params(),
        name="join_sums",
    )(zfrom, mine, *parts)


def shift_x(value, by):
    return lax.ppermute(value, "x", [(i, (i + by) % X) for i in range(X)])


def shift_z(value, by):
    return lax.ppermute(value, "z", [(i, (i + by) % Z) for i in range(Z)])


def swap_core(value):
    return lax.ppermute(value, "c", [(0, 1), (1, 0)])


def share_z(value):
    got = {}
    for by in (4, 3, 2, 1):
        pairs = [(z * C + 1, (z - by) % Z * C + 1) for z in range(Z)]
        if by < 4:
            pairs += [(z * C, (z + by) % Z * C) for z in range(Z)]
        got[by] = lax.ppermute(value, ("z", "c"), pairs)
    return [got[by] for by in (1, 2, 3, 4)]


def column_total(sums, core):
    chip = sums + swap_core(sums)
    got = share_z(chip)
    part = jnp.where(core == 0, chip, 0.0) + ((got[0] + got[1]) + (got[2] + got[3]))
    return part, swap_core(part)


def exchange(parts):
    return lax.all_to_all(parts, ("x", "y"), 0, 0, tiled=True)


def body(teacher_tokens, student_tokens, masked_index, prototypes):
    x, z, core = lax.axis_index("x"), lax.axis_index("z"), lax.axis_index("c")
    xpos = jnp.stack([x, (x + 3) % X, (x + 1) % X, (x + 2) % X]).astype(jnp.int32)
    before = [(z + Z - k) % Z for k in (1, 2, 3)]
    after = [(z + k) % Z for k in (1, 2, 3)]
    far = (z + 4) % Z
    first = [jnp.where(core == 0, b, a) for b, a in zip(before, after)]
    second = [jnp.where(core == 0, a, b) for b, a in zip(before, after)]
    wpos = jnp.stack([z, *first, far, *second, far]).astype(jnp.int32)
    one = jnp.ones((), jnp.int32)
    wvalid = jnp.stack([one] * 4 + [core] + [one] * 3 + [1 - core]).astype(jnp.int32)
    zs = ((z + jnp.arange(Z)) % Z).astype(jnp.int32)
    zfrom = ((z + Z - jnp.arange(Z)) % Z).astype(jnp.int32)
    cores = core[None].astype(jnp.int32)

    other = swap_core(prototypes)
    chip_protos = jnp.where(
        core == 0,
        jnp.concatenate([prototypes, other], axis=0),
        jnp.concatenate([other, prototypes], axis=0),
    )
    from_z = share_z(chip_protos)
    from_core = [swap_core(part) for part in from_z]
    protos_in = [chip_protos, *from_z, *from_core]
    teacher_rows = pick_rows(masked_index, teacher_tokens)
    teacher_in = [teacher_rows] + [shift_x(teacher_rows, by) for by in (1, -1, 2)]
    student_rows = pick_rows(masked_index, student_tokens)
    student_in = [student_rows] + [shift_x(student_rows, by) for by in (1, -1, 2)]

    kern, top, tops, protos = teacher_scores(xpos, wpos, wvalid, teacher_in, protos_in)
    sums, weight = column_pass(True, top, exchange(tops), kern)
    rows, lse = student_totals(xpos, student_in, protos)
    mine, theirs = column_total(sums, core)
    got, _ = row_pass("plain", weight, mine, theirs, kern)
    sums, _ = column_pass(False, weight, exchange(got), kern)
    mine, theirs = column_total(sums, core)
    got, _ = row_pass("lse", weight, mine, theirs, kern, (lse,))
    got = exchange(got)
    lses = got[:, GROUPS:, :]
    sums, _ = column_pass(False, weight, got, kern)
    mine, theirs = column_total(sums, core)
    got, scale = row_pass("loss", weight, mine, theirs, kern, (rows, protos))
    got = exchange(got)
    student, keep, send, loss = gradients(cores, weight, got, lses, scale, kern, rows, protos)

    mine, own, *sends = split_sums(zs, keep, swap_core(send), loss, swap_core(loss))
    parts = [own] + [shift_z(part, by) for by, part in enumerate(sends, 1)]
    student = exchange(student.reshape(PEERS, ROWS // PEERS, D))
    student = jnp.sum(student.astype(F32), axis=0).astype(BF16)
    student = lax.all_to_all(
        jnp.broadcast_to(student[None], (Y,) + student.shape), "y", 0, 0, tiled=True
    )
    grad_weight, loss = join_sums(zfrom, mine, parts)
    return loss[0, 0], student.reshape(OWN_ROWS, D), grad_weight


def solution(mesh):
    named = Mesh(mesh.devices.reshape(X, Z, C, Y), ("x", "z", "c", "y"))
    batch = ("x", "z", "c")
    placed = (
        P(batch, None, None),
        P(batch, None, None),
        P(batch, None),
        P((*batch, "y"), None),
    )
    return jax.shard_map(
        body,
        mesh=named,
        in_specs=placed,
        out_specs=(P(), P(batch, None), P((*batch, "y"), None)),
        check_vma=False,
    )
```

```python
import functools
import math

import jax
import jax.numpy as jnp
from jax import lax
from jax.experimental import pallas as pl
from jax.experimental.pallas import tpu as pltpu
from jax.sharding import Mesh, PartitionSpec as P

X, Z, C, Y = 4, 8, 2, 4
F32, BF16 = jnp.float32, jnp.bfloat16
D = 256
IMAGES = 8
MASKED = 64
OWN_ROWS = 512
OWN_PROTOS = 128
ROWS = X * OWN_ROWS
PROTOS = Z * C * OWN_PROTOS
TOTAL_ROWS = ROWS * Z * C
PEERS = X * Y
LANES = 128
GROUPS = 16
BLOCK = 256
HALVES = BLOCK // LANES
T_SCALE = 1.0 / 0.07
S_SCALE = 1.0 / 0.1
MIB = 1 << 20
UNROLL = 16
LOG2E = math.log2(math.e)
GRAD_SCALE = 1.0 / (0.1 * TOTAL_ROWS)
TRANS_B = (((1,), (1,)), ((), ()))


def whole(shape):
    return pl.BlockSpec(shape, lambda *_: (0,) * len(shape))


def params(mib=32):
    return pltpu.CompilerParams(vmem_limit_bytes=mib * MIB)


def in_vmem(array):
    return pltpu.with_memory_space_constraint(array, pltpu.VMEM)


def down(row):
    return jnp.transpose(jnp.broadcast_to(row, (LANES, LANES)))


def along(column_parts):
    return jnp.sum(jnp.transpose(column_parts), axis=0, keepdims=True)


def spread(ref, first, at, row):
    ref[:, pl.ds(first + at, 1), :] = jnp.broadcast_to(row[None], (ref.shape[0], 1, LANES))


def pick_kernel(index_ref, tokens_ref, out_ref):
    for image in range(IMAGES):
        at = lax.broadcasted_iota(jnp.int32, (D, MASKED), 0)
        chosen = (at == index_ref[image : image + 1, :]).astype(BF16)
        rows = lax.dot_general(
            chosen, tokens_ref[image], (((0,), (0,)), ((), ())), preferred_element_type=F32
        )
        out_ref[image * MASKED : (image + 1) * MASKED, :] = rows.astype(BF16)


def pick_rows(index, tokens):
    return pl.pallas_call(
        pick_kernel,
        out_shape=jax.ShapeDtypeStruct((OWN_ROWS, D), BF16),
        in_specs=[whole(index.shape), whole(tokens.shape)],
        out_specs=whole((OWN_ROWS, D)),
        grid=(1,),
        compiler_params=params(),
        name="pick_rows",
    )(index, tokens)


def place_rows(pieces, out_ref):
    x = lax.axis_index("x")
    for piece, by in zip(pieces, (0, 2, 1, -1)):
        at = lax.rem(x + X - by, X) * OWN_ROWS
        out_ref[pl.ds(pl.multiple_of(at, OWN_ROWS), OWN_ROWS), :] = piece[...]


def place_protos(pieces, out_ref):
    z, core = lax.axis_index("z"), lax.axis_index("c")
    sign = 1 - 2 * core
    chips = [(z, core)]
    chips += [(lax.rem(z + Z - sign * by, Z), core) for by in (1, 2, 3)]
    chips += [(lax.rem(z + Z + sign * by, Z), 1 - core) for by in (1, 2, 3)]
    far = lax.rem(z + Z // 2, Z)
    chips += [(far, core), (far, 1 - core)]
    for piece, (chip, first) in zip(pieces, chips):
        for half in range(piece.shape[0] // OWN_PROTOS):
            which = first if half == 0 else 1 - first
            at = pl.multiple_of((chip * C + which) * OWN_PROTOS, OWN_PROTOS)
            out_ref[pl.ds(at, OWN_PROTOS), :] = piece[half * OWN_PROTOS : (half + 1) * OWN_PROTOS, :]


def teacher_kernel(*refs):
    rows_in, protos_in = refs[:X], refs[X : X + 9]
    kern_ref, top_ref, tops_ref, protos_ref, rows_ref = refs[X + 9 :]
    step = pl.program_id(0)

    @pl.when(step == 0)
    def _():
        place_rows(rows_in, rows_ref)
        place_protos(protos_in, protos_ref)

    rows = rows_ref[pl.ds(pl.multiple_of(step * BLOCK, BLOCK), BLOCK), :]
    scores = lax.dot_general(rows, protos_ref[...], TRANS_B, preferred_element_type=F32)
    top = jnp.max(scores, axis=1, keepdims=True)
    kern_ref[...] = jnp.exp2((scores - top) * (T_SCALE * LOG2E)).astype(BF16)
    for half in range(HALVES):
        part = jnp.broadcast_to(top[half * LANES : (half + 1) * LANES], (LANES, LANES))
        row = jnp.transpose(part)[0:1, :] * T_SCALE
        top_ref[pl.ds(step * HALVES + half, 1), :] = row
        spread(tops_ref, 0, step * HALVES + half, row)


def teacher_scores(rows, protos):
    return pl.pallas_call(
        teacher_kernel,
        out_shape=(
            pltpu.VMEM((ROWS, PROTOS), BF16),
            jax.ShapeDtypeStruct((GROUPS, LANES), F32),
            jax.ShapeDtypeStruct((PEERS, GROUPS, LANES), F32),
            jax.ShapeDtypeStruct((PROTOS, D), BF16),
        ),
        grid=(ROWS // BLOCK,),
        in_specs=[whole(a.shape) for a in rows + protos],
        out_specs=(
            pl.BlockSpec((BLOCK, PROTOS), lambda i: (i, 0)),
            whole((GROUPS, LANES)),
            whole((PEERS, GROUPS, LANES)),
            whole((PROTOS, D)),
        ),
        scratch_shapes=[pltpu.VMEM((ROWS, D), BF16)],
        compiler_params=params(),
        name="teacher_scores",
    )(*rows, *protos)


VMEM_SPEC = pl.BlockSpec(memory_space=pltpu.VMEM)
KERN_BLOCKS = ROWS // BLOCK


def weight_kernel(top_ref, got_ref, out_ref):
    got = got_ref[0]
    for peer in range(1, PEERS):
        got = jnp.maximum(got, got_ref[peer])
    out_ref[...] = jnp.exp(top_ref[...] - got)


def row_weight(top, got):
    return pl.pallas_call(
        weight_kernel,
        out_shape=jax.ShapeDtypeStruct((GROUPS, LANES), F32),
        in_specs=[VMEM_SPEC] * 2,
        out_specs=VMEM_SPEC,
        compiler_params=params(),
        name="row_weight",
    )(top, got)


def column_kernel(first, weight_ref, *refs):
    if first:
        kern_ref, sums_ref, acc_ref = refs
        scaled_ref = weight_ref
    else:
        got_ref, kern_ref, sums_ref, acc_ref, scaled_ref = refs
        scaled_ref[...] = weight_ref[...] / jnp.sum(got_ref[...], axis=0)
    acc_ref[...] = jnp.zeros_like(acc_ref)

    def step(block, carry):
        rows = pl.ds(pl.multiple_of(block * LANES, LANES), LANES)
        weight = down(scaled_ref[pl.ds(block, 1), :])
        for group in range(GROUPS):
            part = kern_ref[rows, group * LANES : (group + 1) * LANES].astype(F32) * weight
            acc_ref[group] += jnp.sum(part.reshape(LANES // 8, 8, LANES), axis=0)
        return carry

    lax.fori_loop(0, GROUPS, step, 0, unroll=UNROLL)
    for group in range(GROUPS):
        spread(sums_ref, 0, group, jnp.sum(acc_ref[group], axis=0, keepdims=True))


def column_pass(weight, kern, got=None):
    first = got is None
    scratch = [pltpu.VMEM((GROUPS, 8, LANES), F32)] + ([] if first else [pltpu.VMEM((GROUPS, LANES), F32)])
    inputs = (weight,) if first else (weight, got)
    return pl.pallas_call(
        functools.partial(column_kernel, first),
        out_shape=jax.ShapeDtypeStruct((Z * C, GROUPS, LANES), F32),
        in_specs=[VMEM_SPEC] * (len(inputs) + 1),
        out_specs=VMEM_SPEC,
        scratch_shapes=scratch,
        compiler_params=params(),
        name="column_pass",
    )(*inputs, in_vmem(kern))


def row_kernel(weight_ref, got_ref, kern_ref, sums_ref, scale_ref):
    scale_ref[...] = 1.0 / jnp.sum(got_ref[...], axis=0)

    def step(block, carry):
        rows = pl.ds(pl.multiple_of(block * LANES, LANES), LANES)
        weight = down(weight_ref[pl.ds(block, 1), :])
        total = jnp.zeros((LANES, LANES), F32)
        for group in range(GROUPS):
            part = kern_ref[rows, group * LANES : (group + 1) * LANES].astype(F32) * weight
            total += part * scale_ref[group : group + 1, :]
        spread(sums_ref, 0, block, along(total))
        return carry

    lax.fori_loop(0, GROUPS, step, 0, unroll=UNROLL)


def row_pass(weight, got, kern):
    return pl.pallas_call(
        row_kernel,
        out_shape=(
            jax.ShapeDtypeStruct((PEERS, GROUPS, LANES), F32),
            jax.ShapeDtypeStruct((GROUPS, LANES), F32),
        ),
        in_specs=[VMEM_SPEC] * 3,
        out_specs=(VMEM_SPEC, VMEM_SPEC),
        compiler_params=params(),
        name="row_pass",
    )(weight, got, in_vmem(kern))


def last_kernel(weight_ref, got_ref, protos_ref, *refs):
    rows_in, (kern_ref, sums_ref, scale_ref, rows_ref, scores_ref) = refs[:X], refs[X:]
    step = pl.program_id(0)

    @pl.when(step == 0)
    def _():
        place_rows(rows_in, rows_ref)
        scale_ref[...] = 1.0 / jnp.sum(got_ref[...], axis=0)

    rows = rows_ref[pl.ds(pl.multiple_of(step * BLOCK, BLOCK), BLOCK), :]
    scores_ref[...] = lax.dot_general(rows, protos_ref[...], TRANS_B, preferred_element_type=F32)
    for half in range(HALVES):
        weight = down(weight_ref[pl.ds(step * HALVES + half, 1), :])
        total = jnp.zeros((LANES, LANES), F32)
        crossed = jnp.zeros((LANES, LANES), F32)
        top = jnp.full((LANES, LANES), -jnp.inf, F32)
        for group in range(GROUPS):
            at = (slice(half * LANES, (half + 1) * LANES), slice(group * LANES, (group + 1) * LANES))
            part = (kern_ref[at].astype(F32) * weight) * scale_ref[group : group + 1, :]
            total += part
            scores = scores_ref[at]
            crossed += part * scores
            top = jnp.maximum(top, scores)
        top = jnp.max(jnp.transpose(top), axis=0, keepdims=True) * (S_SCALE * LOG2E)
        shift = down(top)
        spent = jnp.zeros((LANES, LANES), F32)
        for group in range(GROUPS):
            at = (slice(half * LANES, (half + 1) * LANES), slice(group * LANES, (group + 1) * LANES))
            spent += jnp.exp2(scores_ref[at] * (S_SCALE * LOG2E) - shift)
        spread(sums_ref, 0, step * HALVES + half, along(total))
        spread(sums_ref, GROUPS, step * HALVES + half, along(crossed) * S_SCALE)
        spread(sums_ref, 2 * GROUPS, step * HALVES + half, jnp.log2(along(spent)) + top)


def last_pass(weight, got, protos, rows, kern):
    return pl.pallas_call(
        last_kernel,
        out_shape=(
            jax.ShapeDtypeStruct((PEERS, 3 * GROUPS, LANES), F32),
            jax.ShapeDtypeStruct((GROUPS, LANES), F32),
            jax.ShapeDtypeStruct((ROWS, D), BF16),
        ),
        grid=(ROWS // BLOCK,),
        in_specs=[whole((GROUPS, LANES)), whole((Z * C, GROUPS, LANES)), whole((PROTOS, D))]
        + [whole(r.shape) for r in rows]
        + [pl.BlockSpec((BLOCK, PROTOS), lambda i: (i, 0))],
        out_specs=(
            whole((PEERS, 3 * GROUPS, LANES)),
            whole((GROUPS, LANES)),
            whole((ROWS, D)),
        ),
        scratch_shapes=[pltpu.VMEM((BLOCK, PROTOS), F32)],
        compiler_params=params(),
        name="last_pass",
    )(weight, got, protos, *rows, in_vmem(kern))


def grad_kernel(
    weight_ref, got_ref, scale_ref, kern_ref, rows_ref, protos_ref,
    student_ref, keep_ref, send_ref, loss_ref, scaled_ref, lse_ref, scores_ref, logits_ref, acc_ref,
):
    step = pl.program_id(0)

    @pl.when(step == 0)
    def _():
        sums = jnp.sum(got_ref[:, :GROUPS, :], axis=0)
        crossed = jnp.sum(got_ref[:, GROUPS : 2 * GROUPS, :], axis=0)
        top = got_ref[0, 2 * GROUPS :, :]
        for peer in range(1, PEERS):
            top = jnp.maximum(top, got_ref[peer, 2 * GROUPS :, :])
        total = jnp.zeros_like(top)
        for peer in range(PEERS):
            total += jnp.exp2(got_ref[peer, 2 * GROUPS :, :] - top)
        lse = top + jnp.log2(total)
        lse_ref[...] = lse - math.log2(GRAD_SCALE)
        scaled_ref[...] = weight_ref[...] / sums * GRAD_SCALE
        terms = (lse * math.log(2.0) * sums - crossed) / sums
        terms = jnp.sum(jnp.sum(terms, axis=0, keepdims=True), axis=1, keepdims=True)
        loss_ref[...] = jnp.broadcast_to(terms, (8, LANES))
        acc_ref[...] = jnp.zeros_like(acc_ref)

    rows = rows_ref[...]
    scores_ref[...] = lax.dot_general(rows, protos_ref[...], TRANS_B, preferred_element_type=F32)
    for half in range(HALVES):
        weight = down(scaled_ref[pl.ds(step * HALVES + half, 1), :])
        lse = down(lse_ref[pl.ds(step * HALVES + half, 1), :])
        for group in range(GROUPS):
            at = (slice(half * LANES, (half + 1) * LANES), slice(group * LANES, (group + 1) * LANES))
            target = (kern_ref[at].astype(F32) * weight) * scale_ref[group : group + 1, :]
            prob = jnp.exp2(scores_ref[at] * (S_SCALE * LOG2E) - lse)
            logits_ref[at] = (prob - target).astype(BF16)
    logits = logits_ref[...]
    student_ref[...] = jnp.dot(logits, protos_ref[...], preferred_element_type=F32).astype(BF16)
    acc_ref[...] += jnp.dot(jnp.transpose(rows), logits, preferred_element_type=F32)

    @pl.when(step == pl.num_programs(0) - 1)
    def _():
        core = lax.axis_index("c")
        for z in range(Z):
            for c in range(C):
                first = (z * C + c) * OWN_PROTOS
                part = jnp.transpose(acc_ref[:, first : first + OWN_PROTOS])

                @pl.when(core == c)
                def _(part=part, z=z):
                    keep_ref[z] = part

                @pl.when(core != c)
                def _(part=part, z=z):
                    send_ref[z] = part.astype(BF16)


def gradients(weight, got, scale, kern, rows, protos):
    return pl.pallas_call(
        grad_kernel,
        out_shape=(
            pltpu.HBM((ROWS, D), BF16),
            jax.ShapeDtypeStruct((Z, OWN_PROTOS, D), F32),
            jax.ShapeDtypeStruct((Z, OWN_PROTOS, D), BF16),
            jax.ShapeDtypeStruct((8, LANES), F32),
        ),
        grid=(ROWS // BLOCK,),
        in_specs=[
            whole(weight.shape),
            whole(got.shape),
            whole(scale.shape),
            pl.BlockSpec((BLOCK, PROTOS), lambda i: (i, 0)),
            pl.BlockSpec((BLOCK, D), lambda i: (i, 0)),
            whole((PROTOS, D)),
        ],
        out_specs=(
            pl.BlockSpec((BLOCK, D), lambda i: (i, 0)),
            whole((Z, OWN_PROTOS, D)),
            whole((Z, OWN_PROTOS, D)),
            whole((8, LANES)),
        ),
        scratch_shapes=[
            pltpu.VMEM((GROUPS, LANES), F32),
            pltpu.VMEM((GROUPS, LANES), F32),
            pltpu.VMEM((BLOCK, PROTOS), F32),
            pltpu.VMEM((BLOCK, PROTOS), BF16),
            pltpu.VMEM((D, PROTOS), F32),
        ],
        compiler_params=params(),
        name="gradients",
    )(weight, got, scale, in_vmem(kern), rows, protos)


TAIL = 16


def split_kernel(keep_ref, got_ref, loss_ref, other_ref, mine_ref, *outs):
    value = jnp.broadcast_to((loss_ref[...] + other_ref[...])[0:1, :], (TAIL, LANES))
    high = value.astype(BF16)
    rest = value - high.astype(F32)
    middle = rest.astype(BF16)
    low = (rest - middle.astype(F32)).astype(BF16)
    row = lax.broadcasted_iota(jnp.int32, (TAIL, LANES), 0)
    tail = jnp.where(row == 0, high.astype(F32), jnp.where(row == 1, middle.astype(F32), low.astype(F32)))
    tail = jnp.concatenate([tail, tail], axis=1).astype(BF16)
    for shift, out in enumerate(outs):
        at = lax.rem(lax.axis_index("z") + shift, Z)
        part = keep_ref[at] + got_ref[at].astype(F32)
        if shift == 0:
            mine_ref[...] = part
        out[:OWN_PROTOS, :] = part.astype(BF16)
        out[OWN_PROTOS:, :] = tail


def split_sums(keep, got, loss, other):
    return pl.pallas_call(
        split_kernel,
        out_shape=(jax.ShapeDtypeStruct((OWN_PROTOS, D), F32),)
        + (jax.ShapeDtypeStruct((OWN_PROTOS + TAIL, D), BF16),) * Z,
        in_specs=[VMEM_SPEC] * 4,
        out_specs=(VMEM_SPEC,) * (Z + 1),
        compiler_params=params(),
        name="split_sums",
    )(keep, got, loss, other)


def join_kernel(mine_ref, *refs):
    parts, (out_ref, loss_ref, value_ref) = refs[:Z], refs[Z:]
    total = mine_ref[...]
    for shift, part in enumerate(parts):
        if shift:
            total += part[:OWN_PROTOS, :].astype(F32)
        tail = part[OWN_PROTOS:, :LANES].astype(F32)
        at = lax.rem(lax.axis_index("z") + Z - shift, Z)
        value_ref[pl.ds(at, 1), :] = tail[0:1] + (tail[1:2] + tail[2:3])
    out_ref[...] = total
    loss = value_ref[0:1, :]
    for z in range(1, Z):
        loss = loss + value_ref[z : z + 1, :]
    loss_ref[...] = jnp.broadcast_to(loss, (8, LANES)) * (1.0 / TOTAL_ROWS)


def join_sums(mine, parts):
    return pl.pallas_call(
        join_kernel,
        out_shape=(jax.ShapeDtypeStruct((OWN_PROTOS, D), F32), jax.ShapeDtypeStruct((8, LANES), F32)),
        in_specs=[VMEM_SPEC] * (Z + 1),
        out_specs=(VMEM_SPEC, VMEM_SPEC),
        scratch_shapes=[pltpu.VMEM((Z, LANES), F32)],
        compiler_params=params(),
        name="join_sums",
    )(mine, *parts)


def shift_x(value, by):
    return lax.ppermute(value, "x", [(i, (i + by) % X) for i in range(X)])


def shift_z(value, by):
    return lax.ppermute(value, "z", [(i, (i + by) % Z) for i in range(Z)])


def swap_core(value):
    return lax.ppermute(value, "c", [(0, 1), (1, 0)])


def fan_z(value, by):
    pairs = [(z * C + c, (z + (by if c == 0 else -by)) % Z * C + c) for z in range(Z) for c in range(C)]
    return lax.ppermute(value, ("z", "c"), pairs)


def over_rows(parts):
    return lax.all_to_all(parts, ("x", "y"), 0, 0, tiled=True)


def over_protos(parts):
    return lax.all_to_all(parts, ("z", "c"), 0, 0, tiled=True)


def over_y(parts):
    return lax.all_to_all(parts, "y", 0, 0, tiled=True)


def body(teacher_tokens, student_tokens, masked_index, prototypes):
    teacher_rows = pick_rows(masked_index, teacher_tokens)
    student_rows = pick_rows(masked_index, student_tokens)
    teacher_rows, student_rows, prototypes = lax.optimization_barrier((teacher_rows, student_rows, prototypes))
    other = swap_core(prototypes)
    far_own = shift_z(prototypes, Z // 2)
    teacher_in = [teacher_rows] + [shift_x(teacher_rows, by) for by in (2, 1, -1)]
    chip_protos = jnp.concatenate([prototypes, other], axis=0)
    near = [fan_z(chip_protos, by) for by in (1, 2, 3)]
    protos_in = [chip_protos, *near, *[swap_core(part) for part in near], far_own, swap_core(far_own)]
    student_in = [student_rows] + [shift_x(student_rows, by) for by in (2, 1, -1)]
    kern, top, tops, protos = teacher_scores(teacher_in, protos_in)
    weight = row_weight(top, over_rows(tops))
    weight, student_in = lax.optimization_barrier((weight, student_in))
    sums = column_pass(weight, kern)
    got, _ = row_pass(weight, over_protos(sums), kern)
    sums = column_pass(weight, kern, over_rows(got))
    got, _ = row_pass(weight, over_protos(sums), kern)
    sums = column_pass(weight, kern, over_rows(got))
    got, scale, rows = last_pass(weight, over_protos(sums), protos, student_in, kern)
    student, keep, send, loss = gradients(weight, over_rows(got), scale, kern, rows, protos)

    mine, own, *sends = split_sums(keep, swap_core(send), loss, swap_core(loss))
    parts = [own] + [None] * (Z - 1)
    for by in (4, 3, 5, 2, 6, 1, 7):
        parts[by] = shift_z(sends[by - 1], by)
    student = over_rows(student.reshape(PEERS, ROWS // PEERS, D))
    student, parts[1:] = lax.optimization_barrier((student, parts[1:]))
    student = jnp.sum(student.astype(F32), axis=0).astype(BF16)
    student = over_y(jnp.broadcast_to(student[None], (Y,) + student.shape))
    grad_weight, loss = join_sums(mine, parts)
    return loss[0, 0], student.reshape(OWN_ROWS, D), grad_weight


def solution(mesh):
    named = Mesh(mesh.devices.reshape(X, Z, C, Y), ("x", "z", "c", "y"))
    batch = ("x", "z", "c")
    placed = (
        P(batch, None, None),
        P(batch, None, None),
        P(batch, None),
        P((*batch, "y"), None),
    )
    return jax.shard_map(
        body,
        mesh=named,
        in_specs=placed,
        out_specs=(P(), P(batch, None), P((*batch, "y"), None)),
        check_vma=False,
    )
```

```python
import functools
import math

import jax
import jax.numpy as jnp
from jax import lax
from jax.experimental import pallas as pl
from jax.experimental.pallas import tpu as pltpu
from jax.sharding import Mesh, PartitionSpec as P

X, Z, C, Y = 4, 8, 2, 4
F32, BF16 = jnp.float32, jnp.bfloat16
D = 256
IMAGES = 8
MASKED = 64
OWN_ROWS = 512
OWN_PROTOS = 128
ROWS = X * OWN_ROWS
PROTOS = Z * C * OWN_PROTOS
TOTAL_ROWS = ROWS * Z * C
PEERS = X * Y
LANES = 128
GROUPS = 16
BLOCK = 256
HALVES = BLOCK // LANES
T_SCALE = 1.0 / 0.07
S_SCALE = 1.0 / 0.1
MIB = 1 << 20
UNROLL = 16
LOG2E = math.log2(math.e)
GRAD_SCALE = 1.0 / (0.1 * TOTAL_ROWS)
VMEM_SPEC = pl.BlockSpec(memory_space=pltpu.VMEM)
KERN_BLOCKS = ROWS // BLOCK
TRANS_B = (((1,), (1,)), ((), ()))


def whole(shape):
    return pl.BlockSpec(shape, lambda *_: (0,) * len(shape))


def params(mib=32):
    return pltpu.CompilerParams(vmem_limit_bytes=mib * MIB)


def in_vmem(array):
    return pltpu.with_memory_space_constraint(array, pltpu.VMEM)


def down(row):
    return jnp.transpose(jnp.broadcast_to(row, (LANES, LANES)))


def along(column_parts):
    return jnp.sum(jnp.transpose(column_parts), axis=0, keepdims=True)


def spread(ref, first, at, row):
    ref[:, pl.ds(first + at, 1), :] = jnp.broadcast_to(row[None], (ref.shape[0], 1, LANES))


def pick_kernel(index_ref, tokens_ref, out_ref):
    for image in range(IMAGES):
        at = lax.broadcasted_iota(jnp.int32, (D, MASKED), 0)
        chosen = (at == index_ref[image : image + 1, :]).astype(BF16)
        rows = lax.dot_general(
            chosen, tokens_ref[image], (((0,), (0,)), ((), ())), preferred_element_type=F32
        )
        out_ref[image * MASKED : (image + 1) * MASKED, :] = rows.astype(BF16)


def pick_rows(index, tokens):
    return pl.pallas_call(
        pick_kernel,
        out_shape=jax.ShapeDtypeStruct((OWN_ROWS, D), BF16),
        in_specs=[whole(index.shape), whole(tokens.shape)],
        out_specs=whole((OWN_ROWS, D)),
        grid=(1,),
        compiler_params=params(),
        name="pick_rows",
    )(index, tokens)


def place_rows(pieces, out_ref):
    x = lax.axis_index("x")
    for piece, by in zip(pieces, (0, 2, 1, -1)):
        at = lax.rem(x + X - by, X) * OWN_ROWS
        out_ref[pl.ds(pl.multiple_of(at, OWN_ROWS), OWN_ROWS), :] = piece[...]


def place_protos(pieces, out_ref):
    z, core = lax.axis_index("z"), lax.axis_index("c")
    sign = 1 - 2 * core
    chips = [(z, core)]
    chips += [(lax.rem(z + Z - sign * by, Z), core) for by in (1, 2, 3)]
    chips += [(lax.rem(z + Z + sign * by, Z), 1 - core) for by in (1, 2, 3)]
    far = lax.rem(z + Z // 2, Z)
    chips += [(far, core), (far, 1 - core)]
    for piece, (chip, first) in zip(pieces, chips):
        for half in range(piece.shape[0] // OWN_PROTOS):
            which = first if half == 0 else 1 - first
            at = pl.multiple_of((chip * C + which) * OWN_PROTOS, OWN_PROTOS)
            out_ref[pl.ds(at, OWN_PROTOS), :] = piece[half * OWN_PROTOS : (half + 1) * OWN_PROTOS, :]


def block_rows(block):
    return slice(block * BLOCK, (block + 1) * BLOCK)


def teacher_kernel(*refs):
    rows_in, protos_in = refs[:X], refs[X : X + 9]
    kern_ref, top_ref, tops_ref, protos_ref, rows_ref, *scores_refs = refs[X + 9 :]
    place_rows(rows_in, rows_ref)
    place_protos(protos_in, protos_ref)

    def multiply(block):
        scores_refs[block % 2][...] = lax.dot_general(
            rows_ref[block_rows(block), :], protos_ref[...], TRANS_B, preferred_element_type=F32
        )

    multiply(0)
    for block in range(KERN_BLOCKS):
        if block + 1 < KERN_BLOCKS:
            multiply(block + 1)
        scores_ref = scores_refs[block % 2]
        for half in range(HALVES):
            at = slice(half * LANES, (half + 1) * LANES)
            top = scores_ref[at, :LANES]
            for group in range(1, GROUPS):
                top = jnp.maximum(top, scores_ref[at, group * LANES : (group + 1) * LANES])
            top = jnp.max(jnp.transpose(top), axis=0, keepdims=True)
            shift = down(top)
            for group in range(GROUPS):
                lanes = slice(group * LANES, (group + 1) * LANES)
                value = jnp.exp2((scores_ref[at, lanes] - shift) * (T_SCALE * LOG2E))
                kern_ref[block * BLOCK + half * LANES : block * BLOCK + (half + 1) * LANES, lanes] = value.astype(BF16)
            row = top * T_SCALE
            top_ref[block * HALVES + half : block * HALVES + half + 1, :] = row
            spread(tops_ref, 0, block * HALVES + half, row)


def teacher_scores(rows, protos):
    return pl.pallas_call(
        teacher_kernel,
        out_shape=(
            pltpu.VMEM((ROWS, PROTOS), BF16),
            jax.ShapeDtypeStruct((GROUPS, LANES), F32),
            jax.ShapeDtypeStruct((PEERS, GROUPS, LANES), F32),
            jax.ShapeDtypeStruct((PROTOS, D), BF16),
        ),
        in_specs=[VMEM_SPEC] * (X + 9),
        out_specs=(VMEM_SPEC,) * 4,
        scratch_shapes=[pltpu.VMEM((ROWS, D), BF16)] + [pltpu.VMEM((BLOCK, PROTOS), F32)] * 2,
        compiler_params=params(),
        name="teacher_scores",
    )(*rows, *protos)


def weight_kernel(top_ref, got_ref, out_ref):
    got = got_ref[0]
    for peer in range(1, PEERS):
        got = jnp.maximum(got, got_ref[peer])
    out_ref[...] = jnp.exp(top_ref[...] - got)


def row_weight(top, got):
    return pl.pallas_call(
        weight_kernel,
        out_shape=jax.ShapeDtypeStruct((GROUPS, LANES), F32),
        in_specs=[VMEM_SPEC] * 2,
        out_specs=VMEM_SPEC,
        compiler_params=params(),
        name="row_weight",
    )(top, got)


def column_kernel(first, weight_ref, *refs):
    if first:
        kern_ref, sums_ref, acc_ref = refs
        scaled_ref = weight_ref
    else:
        got_ref, kern_ref, sums_ref, acc_ref, scaled_ref = refs
        scaled_ref[...] = weight_ref[...] / jnp.sum(got_ref[...], axis=0)
    acc_ref[...] = jnp.zeros_like(acc_ref)

    def step(block, carry):
        rows = pl.ds(pl.multiple_of(block * LANES, LANES), LANES)
        weight = down(scaled_ref[pl.ds(block, 1), :])
        for group in range(GROUPS):
            part = kern_ref[rows, group * LANES : (group + 1) * LANES].astype(F32) * weight
            acc_ref[group] += jnp.sum(part.reshape(LANES // 8, 8, LANES), axis=0)
        return carry

    lax.fori_loop(0, GROUPS, step, 0, unroll=UNROLL)
    for group in range(GROUPS):
        spread(sums_ref, 0, group, jnp.sum(acc_ref[group], axis=0, keepdims=True))


def column_pass(weight, kern, got=None):
    first = got is None
    scratch = [pltpu.VMEM((GROUPS, 8, LANES), F32)] + ([] if first else [pltpu.VMEM((GROUPS, LANES), F32)])
    inputs = (weight,) if first else (weight, got)
    return pl.pallas_call(
        functools.partial(column_kernel, first),
        out_shape=jax.ShapeDtypeStruct((Z * C, GROUPS, LANES), F32),
        in_specs=[VMEM_SPEC] * (len(inputs) + 1),
        out_specs=VMEM_SPEC,
        scratch_shapes=scratch,
        compiler_params=params(),
        name="column_pass",
    )(*inputs, in_vmem(kern))


def row_kernel(weight_ref, got_ref, kern_ref, sums_ref, scale_ref):
    scale_ref[...] = 1.0 / jnp.sum(got_ref[...], axis=0)

    def step(block, carry):
        rows = pl.ds(pl.multiple_of(block * LANES, LANES), LANES)
        weight = down(weight_ref[pl.ds(block, 1), :])
        total = jnp.zeros((LANES, LANES), F32)
        for group in range(GROUPS):
            part = kern_ref[rows, group * LANES : (group + 1) * LANES].astype(F32) * weight
            total += part * scale_ref[group : group + 1, :]
        spread(sums_ref, 0, block, along(total))
        return carry

    lax.fori_loop(0, GROUPS, step, 0, unroll=UNROLL)


def row_pass(weight, got, kern):
    return pl.pallas_call(
        row_kernel,
        out_shape=(
            jax.ShapeDtypeStruct((PEERS, GROUPS, LANES), F32),
            jax.ShapeDtypeStruct((GROUPS, LANES), F32),
        ),
        in_specs=[VMEM_SPEC] * 3,
        out_specs=(VMEM_SPEC, VMEM_SPEC),
        compiler_params=params(),
        name="row_pass",
    )(weight, got, in_vmem(kern))


def last_kernel(weight_ref, got_ref, protos_ref, *refs):
    rows_in, (kern_ref, sums_ref, scale_ref, rows_ref, *scores_refs) = refs[:X], refs[X:]
    place_rows(rows_in, rows_ref)
    scale_ref[...] = 1.0 / jnp.sum(got_ref[...], axis=0)

    def multiply(block):
        scores_refs[block % 2][...] = lax.dot_general(
            rows_ref[block_rows(block), :], protos_ref[...], TRANS_B, preferred_element_type=F32
        )

    multiply(0)
    for block in range(KERN_BLOCKS):
        if block + 1 < KERN_BLOCKS:
            multiply(block + 1)
        scores_ref = scores_refs[block % 2]
        for half in range(HALVES):
            group_at = block * HALVES + half
            weight = down(weight_ref[group_at : group_at + 1, :])
            total = jnp.zeros((LANES, LANES), F32)
            crossed = jnp.zeros((LANES, LANES), F32)
            top = jnp.full((LANES, LANES), -jnp.inf, F32)
            at = slice(half * LANES, (half + 1) * LANES)
            kern_at = slice(group_at * LANES, (group_at + 1) * LANES)
            for group in range(GROUPS):
                lanes = slice(group * LANES, (group + 1) * LANES)
                part = (kern_ref[kern_at, lanes].astype(F32) * weight) * scale_ref[group : group + 1, :]
                total += part
                scores = scores_ref[at, lanes]
                crossed += part * scores
                top = jnp.maximum(top, scores)
            top = jnp.max(jnp.transpose(top), axis=0, keepdims=True) * (S_SCALE * LOG2E)
            shift = down(top)
            spent = jnp.zeros((LANES, LANES), F32)
            for group in range(GROUPS):
                lanes = slice(group * LANES, (group + 1) * LANES)
                spent += jnp.exp2(scores_ref[at, lanes] * (S_SCALE * LOG2E) - shift)
            spread(sums_ref, 0, group_at, along(total))
            spread(sums_ref, GROUPS, group_at, along(crossed) * S_SCALE)
            spread(sums_ref, 2 * GROUPS, group_at, jnp.log2(along(spent)) + top)


def last_pass(weight, got, protos, rows, kern):
    return pl.pallas_call(
        last_kernel,
        out_shape=(
            jax.ShapeDtypeStruct((PEERS, 3 * GROUPS, LANES), F32),
            jax.ShapeDtypeStruct((GROUPS, LANES), F32),
            jax.ShapeDtypeStruct((ROWS, D), BF16),
        ),
        in_specs=[VMEM_SPEC] * (X + 4),
        out_specs=(VMEM_SPEC,) * 3,
        scratch_shapes=[pltpu.VMEM((BLOCK, PROTOS), F32)] * 2,
        compiler_params=params(),
        name="last_pass",
    )(weight, got, protos, *rows, in_vmem(kern))


def grad_kernel(
    weight_ref, got_ref, scale_ref, kern_ref, rows_ref, protos_ref, student_ref, keep_ref, send_ref, loss_ref,
    scaled_ref, lse_ref, acc_ref, *scratch,
):
    scores_refs, logits_refs = scratch[:2], scratch[2:]
    sums = jnp.sum(got_ref[:, :GROUPS, :], axis=0)
    crossed = jnp.sum(got_ref[:, GROUPS : 2 * GROUPS, :], axis=0)
    top = got_ref[0, 2 * GROUPS :, :]
    for peer in range(1, PEERS):
        top = jnp.maximum(top, got_ref[peer, 2 * GROUPS :, :])
    total = jnp.zeros_like(top)
    for peer in range(PEERS):
        total += jnp.exp2(got_ref[peer, 2 * GROUPS :, :] - top)
    lse = top + jnp.log2(total)
    lse_ref[...] = lse - math.log2(GRAD_SCALE)
    scaled_ref[...] = weight_ref[...] / sums * GRAD_SCALE
    terms = (lse * math.log(2.0) * sums - crossed) / sums
    terms = jnp.sum(jnp.sum(terms, axis=0, keepdims=True), axis=1, keepdims=True)
    loss_ref[...] = jnp.broadcast_to(terms, (8, LANES))

    def multiply(block):
        scores_refs[block % 2][...] = lax.dot_general(
            rows_ref[block_rows(block), :], protos_ref[...], TRANS_B, preferred_element_type=F32
        )

    def reduce(block):
        logits = logits_refs[block % 2][...]
        student_ref[block_rows(block), :] = jnp.dot(
            logits, protos_ref[...], preferred_element_type=F32
        ).astype(BF16)
        part = jnp.dot(jnp.transpose(rows_ref[block_rows(block), :]), logits, preferred_element_type=F32)
        if block == 0:
            acc_ref[...] = part
        else:
            acc_ref[...] += part

    multiply(0)
    for block in range(KERN_BLOCKS):
        if block + 1 < KERN_BLOCKS:
            multiply(block + 1)
        if block > 0:
            reduce(block - 1)
        for half in range(HALVES):
            group_at = block * HALVES + half
            weight = down(scaled_ref[group_at : group_at + 1, :])
            lse = down(lse_ref[group_at : group_at + 1, :])
            kern_at = slice(group_at * LANES, (group_at + 1) * LANES)
            for group in range(GROUPS):
                lanes = slice(group * LANES, (group + 1) * LANES)
                at = (slice(half * LANES, (half + 1) * LANES), lanes)
                target = (kern_ref[kern_at, lanes].astype(F32) * weight) * scale_ref[group : group + 1, :]
                prob = jnp.exp2(scores_refs[block % 2][at] * (S_SCALE * LOG2E) - lse)
                logits_refs[block % 2][at] = (prob - target).astype(BF16)
    reduce(KERN_BLOCKS - 1)

    core = lax.axis_index("c")
    for z in range(Z):
        for c in range(C):
            first = (z * C + c) * OWN_PROTOS
            part = jnp.transpose(acc_ref[:, first : first + OWN_PROTOS])

            @pl.when(core == c)
            def _(part=part, z=z):
                keep_ref[z] = part

            @pl.when(core != c)
            def _(part=part, z=z):
                send_ref[z] = part.astype(BF16)


def gradients(weight, got, scale, kern, rows, protos):
    return pl.pallas_call(
        grad_kernel,
        out_shape=(
            pltpu.HBM((ROWS, D), BF16),
            jax.ShapeDtypeStruct((Z, OWN_PROTOS, D), F32),
            jax.ShapeDtypeStruct((Z, OWN_PROTOS, D), BF16),
            jax.ShapeDtypeStruct((8, LANES), F32),
        ),
        in_specs=[VMEM_SPEC] * 6,
        out_specs=(VMEM_SPEC,) * 4,
        scratch_shapes=[
            pltpu.VMEM((GROUPS, LANES), F32),
            pltpu.VMEM((GROUPS, LANES), F32),
            pltpu.VMEM((D, PROTOS), F32),
        ]
        + [pltpu.VMEM((BLOCK, PROTOS), F32)] * 2
        + [pltpu.VMEM((BLOCK, PROTOS), BF16)] * 2,
        compiler_params=params(),
        name="gradients",
    )(weight, got, scale, in_vmem(kern), rows, protos)


TAIL = 16


def split_kernel(keep_ref, got_ref, loss_ref, other_ref, mine_ref, *outs):
    value = jnp.broadcast_to((loss_ref[...] + other_ref[...])[0:1, :], (TAIL, LANES))
    high = value.astype(BF16)
    rest = value - high.astype(F32)
    middle = rest.astype(BF16)
    low = (rest - middle.astype(F32)).astype(BF16)
    row = lax.broadcasted_iota(jnp.int32, (TAIL, LANES), 0)
    tail = jnp.where(row == 0, high.astype(F32), jnp.where(row == 1, middle.astype(F32), low.astype(F32)))
    tail = jnp.concatenate([tail, tail], axis=1).astype(BF16)
    for shift, out in enumerate(outs):
        at = lax.rem(lax.axis_index("z") + shift, Z)
        part = keep_ref[at] + got_ref[at].astype(F32)
        if shift == 0:
            mine_ref[...] = part
        out[:OWN_PROTOS, :] = part.astype(BF16)
        out[OWN_PROTOS:, :] = tail


def split_sums(keep, got, loss, other):
    return pl.pallas_call(
        split_kernel,
        out_shape=(jax.ShapeDtypeStruct((OWN_PROTOS, D), F32),)
        + (jax.ShapeDtypeStruct((OWN_PROTOS + TAIL, D), BF16),) * Z,
        in_specs=[VMEM_SPEC] * 4,
        out_specs=(VMEM_SPEC,) * (Z + 1),
        compiler_params=params(),
        name="split_sums",
    )(keep, got, loss, other)


def join_kernel(mine_ref, *refs):
    parts, (out_ref, loss_ref, value_ref) = refs[:Z], refs[Z:]
    total = mine_ref[...]
    for shift, part in enumerate(parts):
        if shift:
            total += part[:OWN_PROTOS, :].astype(F32)
        tail = part[OWN_PROTOS:, :LANES].astype(F32)
        at = lax.rem(lax.axis_index("z") + Z - shift, Z)
        value_ref[pl.ds(at, 1), :] = tail[0:1] + (tail[1:2] + tail[2:3])
    out_ref[...] = total
    loss = value_ref[0:1, :]
    for z in range(1, Z):
        loss = loss + value_ref[z : z + 1, :]
    loss_ref[...] = jnp.broadcast_to(loss, (8, LANES)) * (1.0 / TOTAL_ROWS)


def join_sums(mine, parts):
    return pl.pallas_call(
        join_kernel,
        out_shape=(jax.ShapeDtypeStruct((OWN_PROTOS, D), F32), jax.ShapeDtypeStruct((8, LANES), F32)),
        in_specs=[VMEM_SPEC] * (Z + 1),
        out_specs=(VMEM_SPEC, VMEM_SPEC),
        scratch_shapes=[pltpu.VMEM((Z, LANES), F32)],
        compiler_params=params(),
        name="join_sums",
    )(mine, *parts)


def shift_x(value, by):
    return lax.ppermute(value, "x", [(i, (i + by) % X) for i in range(X)])


def shift_z(value, by):
    return lax.ppermute(value, "z", [(i, (i + by) % Z) for i in range(Z)])


def swap_core(value):
    return lax.ppermute(value, "c", [(0, 1), (1, 0)])


def fan_z(value, by):
    pairs = [(z * C + c, (z + (by if c == 0 else -by)) % Z * C + c) for z in range(Z) for c in range(C)]
    return lax.ppermute(value, ("z", "c"), pairs)


def over_rows(parts):
    return lax.all_to_all(parts, ("x", "y"), 0, 0, tiled=True)


def over_protos(parts):
    return lax.all_to_all(parts, ("z", "c"), 0, 0, tiled=True)


def over_y(parts):
    return lax.all_to_all(parts, "y", 0, 0, tiled=True)


def body(teacher_tokens, student_tokens, masked_index, prototypes):
    teacher_rows = pick_rows(masked_index, teacher_tokens)
    chip_protos = jnp.concatenate([prototypes, swap_core(prototypes)], axis=0)
    chip_protos, prototypes, teacher_rows = lax.optimization_barrier((chip_protos, prototypes, teacher_rows))
    near = [fan_z(chip_protos, by) for by in (3, 2, 1)]
    far_own = shift_z(prototypes, Z // 2)
    teacher_in = [teacher_rows] + [shift_x(teacher_rows, by) for by in (2, 1, -1)]
    near, far_own, teacher_in, student_tokens = lax.optimization_barrier(
        (near[::-1], far_own, teacher_in, student_tokens)
    )
    student_rows = pick_rows(masked_index, student_tokens)
    student_in = [student_rows] + [shift_x(student_rows, by) for by in (2, 1, -1)]
    protos_in = [chip_protos, *near, *[swap_core(part) for part in near], far_own, swap_core(far_own)]

    kern, top, tops, protos = teacher_scores(teacher_in, protos_in)
    weight = row_weight(top, over_rows(tops))
    weight, student_in = lax.optimization_barrier((weight, student_in))
    sums = column_pass(weight, kern)
    got, _ = row_pass(weight, over_protos(sums), kern)
    sums = column_pass(weight, kern, over_rows(got))
    got, _ = row_pass(weight, over_protos(sums), kern)
    sums = column_pass(weight, kern, over_rows(got))
    got, scale, rows = last_pass(weight, over_protos(sums), protos, student_in, kern)
    student, keep, send, loss = gradients(weight, over_rows(got), scale, kern, rows, protos)

    mine, own, *sends = split_sums(keep, swap_core(send), loss, swap_core(loss))
    parts = [own] + [None] * (Z - 1)
    for by in (4, 3, 5, 2, 6, 1, 7):
        parts[by] = shift_z(sends[by - 1], by)
    student = over_rows(student.reshape(PEERS, ROWS // PEERS, D))
    student, parts[1:] = lax.optimization_barrier((student, parts[1:]))
    student = jnp.sum(student.astype(F32), axis=0).astype(BF16)
    student = over_y(jnp.broadcast_to(student[None], (Y,) + student.shape))
    grad_weight, loss = join_sums(mine, parts)
    return loss[0, 0], student.reshape(OWN_ROWS, D), grad_weight


def solution(mesh):
    named = Mesh(mesh.devices.reshape(X, Z, C, Y), ("x", "z", "c", "y"))
    batch = ("x", "z", "c")
    placed = (
        P(batch, None, None),
        P(batch, None, None),
        P(batch, None),
        P((*batch, "y"), None),
    )
    return jax.shard_map(
        body,
        mesh=named,
        in_specs=placed,
        out_specs=(P(), P(batch, None), P((*batch, "y"), None)),
        check_vma=False,
    )
```

```python
import functools
import math

import jax
import jax.numpy as jnp
from jax import lax
from jax.experimental import pallas as pl
from jax.experimental.pallas import tpu as pltpu
from jax.sharding import Mesh, PartitionSpec as P

X, Z, C, Y = 4, 8, 2, 4
F32, BF16 = jnp.float32, jnp.bfloat16
D = 256
IMAGES = 8
MASKED = 64
OWN_ROWS = 512
OWN_PROTOS = 128
ROWS = X * OWN_ROWS
PROTOS = Z * C * OWN_PROTOS
TOTAL_ROWS = ROWS * Z * C
PEERS = X * Y
LANES = 128
GROUPS = 16
BLOCK = 256
HALVES = BLOCK // LANES
T_SCALE = 1.0 / 0.07
S_SCALE = 1.0 / 0.1
MIB = 1 << 20
UNROLL = 8
LOG2E = math.log2(math.e)
GRAD_SCALE = 1.0 / (0.1 * TOTAL_ROWS)
VMEM_SPEC = pl.BlockSpec(memory_space=pltpu.VMEM)
KERN_BLOCKS = ROWS // BLOCK
TRANS_B = (((1,), (1,)), ((), ()))


def whole(shape):
    return pl.BlockSpec(shape, lambda *_: (0,) * len(shape))


def params(mib=32):
    return pltpu.CompilerParams(vmem_limit_bytes=mib * MIB)


def in_vmem(array):
    return pltpu.with_memory_space_constraint(array, pltpu.VMEM)


def down(row):
    return jnp.transpose(jnp.broadcast_to(row, (LANES, LANES)))


def along(column_parts):
    return jnp.sum(jnp.transpose(column_parts), axis=0, keepdims=True)


def spread(ref, first, at, row):
    ref[:, pl.ds(first + at, 1), :] = jnp.broadcast_to(row[None], (ref.shape[0], 1, LANES))


def pick_kernel(index_ref, tokens_ref, out_ref):
    for image in range(IMAGES):
        at = lax.broadcasted_iota(jnp.int32, (D, MASKED), 0)
        chosen = (at == index_ref[image : image + 1, :]).astype(BF16)
        rows = lax.dot_general(
            chosen, tokens_ref[image], (((0,), (0,)), ((), ())), preferred_element_type=F32
        )
        out_ref[image * MASKED : (image + 1) * MASKED, :] = rows.astype(BF16)


def pick_rows(index, tokens):
    return pl.pallas_call(
        pick_kernel,
        out_shape=jax.ShapeDtypeStruct((OWN_ROWS, D), BF16),
        in_specs=[whole(index.shape), whole(tokens.shape)],
        out_specs=whole((OWN_ROWS, D)),
        grid=(1,),
        compiler_params=params(),
        name="pick_rows",
    )(index, tokens)


def place_rows(pieces, out_ref):
    x = lax.axis_index("x")
    for piece, by in zip(pieces, (0, 2, 1, -1)):
        at = lax.rem(x + X - by, X) * OWN_ROWS
        out_ref[pl.ds(pl.multiple_of(at, OWN_ROWS), OWN_ROWS), :] = piece[...]


def place_protos(pieces, out_ref):
    z, core = lax.axis_index("z"), lax.axis_index("c")
    sign = 1 - 2 * core
    chips = [(z, core)]
    chips += [(lax.rem(z + Z - sign * by, Z), core) for by in (1, 2, 3)]
    chips += [(lax.rem(z + Z + sign * by, Z), 1 - core) for by in (1, 2, 3)]
    far = lax.rem(z + Z // 2, Z)
    chips += [(far, core), (far, 1 - core)]
    for piece, (chip, first) in zip(pieces, chips):
        for half in range(piece.shape[0] // OWN_PROTOS):
            which = first if half == 0 else 1 - first
            at = pl.multiple_of((chip * C + which) * OWN_PROTOS, OWN_PROTOS)
            out_ref[pl.ds(at, OWN_PROTOS), :] = piece[half * OWN_PROTOS : (half + 1) * OWN_PROTOS, :]


def block_rows(block):
    return pl.ds(pl.multiple_of(block * BLOCK, BLOCK), BLOCK)


def in_pairs(multiply, work):
    multiply(0, 0)

    def step(pair, carry):
        for parity in range(2):
            block = 2 * pair + parity
            multiply(jnp.minimum(block + 1, KERN_BLOCKS - 1), 1 - parity)
            work(block, parity)
        return carry

    lax.fori_loop(0, KERN_BLOCKS // 2, step, 0)


def teacher_kernel(*refs):
    rows_in, protos_in = refs[:X], refs[X : X + 9]
    kern_ref, top_ref, tops_ref, protos_ref, rows_ref, *scores_refs = refs[X + 9 :]
    place_rows(rows_in, rows_ref)
    place_protos(protos_in, protos_ref)

    def multiply(block, parity):
        scores_refs[parity][...] = lax.dot_general(
            rows_ref[block_rows(block), :], protos_ref[...], TRANS_B, preferred_element_type=F32
        )

    def work(block, parity):
        scores_ref = scores_refs[parity]
        for half in range(HALVES):
            at = slice(half * LANES, (half + 1) * LANES)
            group_at = block * HALVES + half
            kern_at = pl.ds(pl.multiple_of(group_at * LANES, LANES), LANES)
            top = scores_ref[at, :LANES]
            for group in range(1, GROUPS):
                top = jnp.maximum(top, scores_ref[at, group * LANES : (group + 1) * LANES])
            top = jnp.max(jnp.transpose(top), axis=0, keepdims=True)
            shift = down(top)
            for group in range(GROUPS):
                lanes = slice(group * LANES, (group + 1) * LANES)
                value = jnp.exp2((scores_ref[at, lanes] - shift) * (T_SCALE * LOG2E))
                kern_ref[kern_at, lanes] = value.astype(BF16)
            row = top * T_SCALE
            top_ref[pl.ds(group_at, 1), :] = row
            spread(tops_ref, 0, group_at, row)

    in_pairs(multiply, work)


def teacher_scores(rows, protos):
    return pl.pallas_call(
        teacher_kernel,
        out_shape=(
            pltpu.VMEM((ROWS, PROTOS), BF16),
            jax.ShapeDtypeStruct((GROUPS, LANES), F32),
            jax.ShapeDtypeStruct((PEERS, GROUPS, LANES), F32),
            jax.ShapeDtypeStruct((PROTOS, D), BF16),
        ),
        in_specs=[VMEM_SPEC] * (X + 9),
        out_specs=(VMEM_SPEC,) * 4,
        scratch_shapes=[pltpu.VMEM((ROWS, D), BF16)] + [pltpu.VMEM((BLOCK, PROTOS), F32)] * 2,
        compiler_params=params(),
        name="teacher_scores",
    )(*rows, *protos)


def weight_kernel(top_ref, got_ref, out_ref):
    got = got_ref[0]
    for peer in range(1, PEERS):
        got = jnp.maximum(got, got_ref[peer])
    out_ref[...] = jnp.exp(top_ref[...] - got)


def row_weight(top, got):
    return pl.pallas_call(
        weight_kernel,
        out_shape=jax.ShapeDtypeStruct((GROUPS, LANES), F32),
        in_specs=[VMEM_SPEC] * 2,
        out_specs=VMEM_SPEC,
        compiler_params=params(),
        name="row_weight",
    )(top, got)


def column_kernel(first, weight_ref, *refs):
    if first:
        kern_ref, sums_ref, acc_ref = refs
        scaled_ref = weight_ref
    else:
        got_ref, kern_ref, sums_ref, acc_ref, scaled_ref = refs
        scaled_ref[...] = weight_ref[...] / jnp.sum(got_ref[...], axis=0)
    acc_ref[...] = jnp.zeros_like(acc_ref)

    def step(block, carry):
        rows = pl.ds(pl.multiple_of(block * LANES, LANES), LANES)
        weight = down(scaled_ref[pl.ds(block, 1), :])
        for group in range(GROUPS):
            part = kern_ref[rows, group * LANES : (group + 1) * LANES].astype(F32) * weight
            acc_ref[group] += jnp.sum(part.reshape(LANES // 8, 8, LANES), axis=0)
        return carry

    lax.fori_loop(0, GROUPS, step, 0, unroll=UNROLL)
    for group in range(GROUPS):
        spread(sums_ref, 0, group, jnp.sum(acc_ref[group], axis=0, keepdims=True))


def column_pass(weight, kern, got=None):
    first = got is None
    scratch = [pltpu.VMEM((GROUPS, 8, LANES), F32)] + ([] if first else [pltpu.VMEM((GROUPS, LANES), F32)])
    inputs = (weight,) if first else (weight, got)
    return pl.pallas_call(
        functools.partial(column_kernel, first),
        out_shape=jax.ShapeDtypeStruct((Z * C, GROUPS, LANES), F32),
        in_specs=[VMEM_SPEC] * (len(inputs) + 1),
        out_specs=VMEM_SPEC,
        scratch_shapes=scratch,
        compiler_params=params(),
        name="column_pass",
    )(*inputs, in_vmem(kern))


def row_kernel(weight_ref, got_ref, kern_ref, sums_ref, scale_ref):
    scale_ref[...] = 1.0 / jnp.sum(got_ref[...], axis=0)

    def step(block, carry):
        rows = pl.ds(pl.multiple_of(block * LANES, LANES), LANES)
        weight = down(weight_ref[pl.ds(block, 1), :])
        total = jnp.zeros((LANES, LANES), F32)
        for group in range(GROUPS):
            part = kern_ref[rows, group * LANES : (group + 1) * LANES].astype(F32) * weight
            total += part * scale_ref[group : group + 1, :]
        spread(sums_ref, 0, block, along(total))
        return carry

    lax.fori_loop(0, GROUPS, step, 0, unroll=UNROLL)


def row_pass(weight, got, kern):
    return pl.pallas_call(
        row_kernel,
        out_shape=(
            jax.ShapeDtypeStruct((PEERS, GROUPS, LANES), F32),
            jax.ShapeDtypeStruct((GROUPS, LANES), F32),
        ),
        in_specs=[VMEM_SPEC] * 3,
        out_specs=(VMEM_SPEC, VMEM_SPEC),
        compiler_params=params(),
        name="row_pass",
    )(weight, got, in_vmem(kern))


def last_kernel(weight_ref, got_ref, protos_ref, *refs):
    rows_in, (kern_ref, sums_ref, scale_ref, rows_ref, *scores_refs) = refs[:X], refs[X:]
    place_rows(rows_in, rows_ref)
    scale_ref[...] = 1.0 / jnp.sum(got_ref[...], axis=0)

    def multiply(block, parity):
        scores_refs[parity][...] = lax.dot_general(
            rows_ref[block_rows(block), :], protos_ref[...], TRANS_B, preferred_element_type=F32
        )

    def work(block, parity):
        scores_ref = scores_refs[parity]
        for half in range(HALVES):
            group_at = block * HALVES + half
            weight = down(weight_ref[pl.ds(group_at, 1), :])
            total = jnp.zeros((LANES, LANES), F32)
            crossed = jnp.zeros((LANES, LANES), F32)
            top = jnp.full((LANES, LANES), -jnp.inf, F32)
            at = slice(half * LANES, (half + 1) * LANES)
            kern_at = pl.ds(pl.multiple_of(group_at * LANES, LANES), LANES)
            for group in range(GROUPS):
                lanes = slice(group * LANES, (group + 1) * LANES)
                part = (kern_ref[kern_at, lanes].astype(F32) * weight) * scale_ref[group : group + 1, :]
                total += part
                scores = scores_ref[at, lanes]
                crossed += part * scores
                top = jnp.maximum(top, scores)
            top = jnp.max(jnp.transpose(top), axis=0, keepdims=True) * (S_SCALE * LOG2E)
            shift = down(top)
            spent = jnp.zeros((LANES, LANES), F32)
            for group in range(GROUPS):
                lanes = slice(group * LANES, (group + 1) * LANES)
                spent += jnp.exp2(scores_ref[at, lanes] * (S_SCALE * LOG2E) - shift)
            spread(sums_ref, 0, group_at, along(total))
            spread(sums_ref, GROUPS, group_at, along(crossed) * S_SCALE)
            spread(sums_ref, 2 * GROUPS, group_at, jnp.log2(along(spent)) + top)

    in_pairs(multiply, work)


def last_pass(weight, got, protos, rows, kern):
    return pl.pallas_call(
        last_kernel,
        out_shape=(
            jax.ShapeDtypeStruct((PEERS, 3 * GROUPS, LANES), F32),
            jax.ShapeDtypeStruct((GROUPS, LANES), F32),
            jax.ShapeDtypeStruct((ROWS, D), BF16),
        ),
        in_specs=[VMEM_SPEC] * (X + 4),
        out_specs=(VMEM_SPEC,) * 3,
        scratch_shapes=[pltpu.VMEM((BLOCK, PROTOS), F32)] * 2,
        compiler_params=params(),
        name="last_pass",
    )(weight, got, protos, *rows, in_vmem(kern))


def grad_kernel(
    weight_ref, got_ref, scale_ref, kern_ref, rows_ref, protos_ref, student_ref, keep_ref, send_ref, loss_ref,
    scaled_ref, lse_ref, acc_ref, *scratch,
):
    scores_refs, logits_refs = scratch[:2], scratch[2:]
    sums = jnp.sum(got_ref[:, :GROUPS, :], axis=0)
    crossed = jnp.sum(got_ref[:, GROUPS : 2 * GROUPS, :], axis=0)
    top = got_ref[0, 2 * GROUPS :, :]
    for peer in range(1, PEERS):
        top = jnp.maximum(top, got_ref[peer, 2 * GROUPS :, :])
    total = jnp.zeros_like(top)
    for peer in range(PEERS):
        total += jnp.exp2(got_ref[peer, 2 * GROUPS :, :] - top)
    lse = top + jnp.log2(total)
    lse_ref[...] = lse - math.log2(GRAD_SCALE)
    scaled_ref[...] = weight_ref[...] / sums * GRAD_SCALE
    terms = (lse * math.log(2.0) * sums - crossed) / sums
    terms = jnp.sum(jnp.sum(terms, axis=0, keepdims=True), axis=1, keepdims=True)
    loss_ref[...] = jnp.broadcast_to(terms, (8, LANES))

    logits_refs[1][...] = jnp.zeros((BLOCK, PROTOS), BF16)
    acc_ref[...] = jnp.zeros_like(acc_ref)

    def multiply(block, parity):
        scores_refs[parity][...] = lax.dot_general(
            rows_ref[block_rows(block), :], protos_ref[...], TRANS_B, preferred_element_type=F32
        )

    def reduce(block, parity):
        logits = logits_refs[parity][...]
        student_ref[block_rows(block), :] = jnp.dot(
            logits, protos_ref[...], preferred_element_type=F32
        ).astype(BF16)
        acc_ref[...] += jnp.dot(
            jnp.transpose(rows_ref[block_rows(block), :]), logits, preferred_element_type=F32
        )

    def work(block, parity):
        reduce(jnp.maximum(block - 1, 0), 1 - parity)
        for half in range(HALVES):
            group_at = block * HALVES + half
            weight = down(scaled_ref[pl.ds(group_at, 1), :])
            lse = down(lse_ref[pl.ds(group_at, 1), :])
            kern_at = pl.ds(pl.multiple_of(group_at * LANES, LANES), LANES)
            for group in range(GROUPS):
                lanes = slice(group * LANES, (group + 1) * LANES)
                at = (slice(half * LANES, (half + 1) * LANES), lanes)
                target = (kern_ref[kern_at, lanes].astype(F32) * weight) * scale_ref[group : group + 1, :]
                prob = jnp.exp2(scores_refs[parity][at] * (S_SCALE * LOG2E) - lse)
                logits_refs[parity][at] = (prob - target).astype(BF16)

    in_pairs(multiply, work)
    reduce(KERN_BLOCKS - 1, 1)

    core = lax.axis_index("c")
    for z in range(Z):
        for c in range(C):
            first = (z * C + c) * OWN_PROTOS
            part = jnp.transpose(acc_ref[:, first : first + OWN_PROTOS])

            @pl.when(core == c)
            def _(part=part, z=z):
                keep_ref[z] = part

            @pl.when(core != c)
            def _(part=part, z=z):
                send_ref[z] = part.astype(BF16)


def gradients(weight, got, scale, kern, rows, protos):
    return pl.pallas_call(
        grad_kernel,
        out_shape=(
            pltpu.HBM((ROWS, D), BF16),
            jax.ShapeDtypeStruct((Z, OWN_PROTOS, D), F32),
            jax.ShapeDtypeStruct((Z, OWN_PROTOS, D), BF16),
            jax.ShapeDtypeStruct((8, LANES), F32),
        ),
        in_specs=[VMEM_SPEC] * 6,
        out_specs=(VMEM_SPEC,) * 4,
        scratch_shapes=[
            pltpu.VMEM((GROUPS, LANES), F32),
            pltpu.VMEM((GROUPS, LANES), F32),
            pltpu.VMEM((D, PROTOS), F32),
        ]
        + [pltpu.VMEM((BLOCK, PROTOS), F32)] * 2
        + [pltpu.VMEM((BLOCK, PROTOS), BF16)] * 2,
        compiler_params=params(),
        name="gradients",
    )(weight, got, scale, in_vmem(kern), rows, protos)


TAIL = 16


def split_kernel(keep_ref, got_ref, loss_ref, other_ref, mine_ref, *outs):
    value = jnp.broadcast_to((loss_ref[...] + other_ref[...])[0:1, :], (TAIL, LANES))
    high = value.astype(BF16)
    rest = value - high.astype(F32)
    middle = rest.astype(BF16)
    low = (rest - middle.astype(F32)).astype(BF16)
    row = lax.broadcasted_iota(jnp.int32, (TAIL, LANES), 0)
    tail = jnp.where(row == 0, high.astype(F32), jnp.where(row == 1, middle.astype(F32), low.astype(F32)))
    tail = jnp.concatenate([tail, tail], axis=1).astype(BF16)
    for shift, out in enumerate(outs):
        at = lax.rem(lax.axis_index("z") + shift, Z)
        part = keep_ref[at] + got_ref[at].astype(F32)
        if shift == 0:
            mine_ref[...] = part
        out[:OWN_PROTOS, :] = part.astype(BF16)
        out[OWN_PROTOS:, :] = tail


def split_sums(keep, got, loss, other):
    return pl.pallas_call(
        split_kernel,
        out_shape=(jax.ShapeDtypeStruct((OWN_PROTOS, D), F32),)
        + (jax.ShapeDtypeStruct((OWN_PROTOS + TAIL, D), BF16),) * Z,
        in_specs=[VMEM_SPEC] * 4,
        out_specs=(VMEM_SPEC,) * (Z + 1),
        compiler_params=params(),
        name="split_sums",
    )(keep, got, loss, other)


def join_kernel(mine_ref, *refs):
    parts, (out_ref, loss_ref, value_ref) = refs[:Z], refs[Z:]
    total = mine_ref[...]
    for shift, part in enumerate(parts):
        if shift:
            total += part[:OWN_PROTOS, :].astype(F32)
        tail = part[OWN_PROTOS:, :LANES].astype(F32)
        at = lax.rem(lax.axis_index("z") + Z - shift, Z)
        value_ref[pl.ds(at, 1), :] = tail[0:1] + (tail[1:2] + tail[2:3])
    out_ref[...] = total
    loss = value_ref[0:1, :]
    for z in range(1, Z):
        loss = loss + value_ref[z : z + 1, :]
    loss_ref[...] = jnp.broadcast_to(loss, (8, LANES)) * (1.0 / TOTAL_ROWS)


def join_sums(mine, parts):
    return pl.pallas_call(
        join_kernel,
        out_shape=(jax.ShapeDtypeStruct((OWN_PROTOS, D), F32), jax.ShapeDtypeStruct((8, LANES), F32)),
        in_specs=[VMEM_SPEC] * (Z + 1),
        out_specs=(VMEM_SPEC, VMEM_SPEC),
        scratch_shapes=[pltpu.VMEM((Z, LANES), F32)],
        compiler_params=params(),
        name="join_sums",
    )(mine, *parts)


def shift_x(value, by):
    return lax.ppermute(value, "x", [(i, (i + by) % X) for i in range(X)])


def shift_z(value, by):
    return lax.ppermute(value, "z", [(i, (i + by) % Z) for i in range(Z)])


def swap_core(value):
    return lax.ppermute(value, "c", [(0, 1), (1, 0)])


def fan_z(value, by):
    pairs = [(z * C + c, (z + (by if c == 0 else -by)) % Z * C + c) for z in range(Z) for c in range(C)]
    return lax.ppermute(value, ("z", "c"), pairs)


def over_rows(parts):
    return lax.all_to_all(parts, ("x", "y"), 0, 0, tiled=True)


def over_protos(parts):
    return lax.all_to_all(parts, ("z", "c"), 0, 0, tiled=True)


def over_y(parts):
    return lax.all_to_all(parts, "y", 0, 0, tiled=True)


def body(teacher_tokens, student_tokens, masked_index, prototypes):
    teacher_rows = pick_rows(masked_index, teacher_tokens)
    teacher_rows, prototypes = lax.optimization_barrier((teacher_rows, prototypes))
    other = swap_core(prototypes)
    far_own = shift_z(prototypes, Z // 2)
    teacher_in = [teacher_rows] + [shift_x(teacher_rows, by) for by in (2, 1, -1)]
    chip_protos = jnp.concatenate([prototypes, other], axis=0)
    near = [fan_z(chip_protos, by) for by in (1, 2, 3)]
    far_own, near[2], student_tokens = lax.optimization_barrier((far_own, near[2], student_tokens))
    student_rows = pick_rows(masked_index, student_tokens)
    student_in = [student_rows] + [shift_x(student_rows, by) for by in (2, 1, -1)]
    protos_in = [chip_protos, *near, *[swap_core(part) for part in near], far_own, swap_core(far_own)]

    kern, top, tops, protos = teacher_scores(teacher_in, protos_in)
    weight = row_weight(top, over_rows(tops))
    weight, student_in = lax.optimization_barrier((weight, student_in))
    sums = column_pass(weight, kern)
    got, _ = row_pass(weight, over_protos(sums), kern)
    sums = column_pass(weight, kern, over_rows(got))
    got, _ = row_pass(weight, over_protos(sums), kern)
    sums = column_pass(weight, kern, over_rows(got))
    got, scale, rows = last_pass(weight, over_protos(sums), protos, student_in, kern)
    student, keep, send, loss = gradients(weight, over_rows(got), scale, kern, rows, protos)

    mine, own, *sends = split_sums(keep, swap_core(send), loss, swap_core(loss))
    parts = [own] + [None] * (Z - 1)
    for by in (4, 3, 5, 2, 6, 1, 7):
        parts[by] = shift_z(sends[by - 1], by)
    student = over_rows(student.reshape(PEERS, ROWS // PEERS, D))
    student, parts[2:6] = lax.optimization_barrier((student, parts[2:6]))
    student = jnp.sum(student.astype(F32), axis=0).astype(BF16)
    student = over_y(jnp.broadcast_to(student[None], (Y,) + student.shape))
    grad_weight, loss = join_sums(mine, parts)
    return loss[0, 0], student.reshape(OWN_ROWS, D), grad_weight


def solution(mesh):
    named = Mesh(mesh.devices.reshape(X, Z, C, Y), ("x", "z", "c", "y"))
    batch = ("x", "z", "c")
    placed = (
        P(batch, None, None),
        P(batch, None, None),
        P(batch, None),
        P((*batch, "y"), None),
    )
    return jax.shard_map(
        body,
        mesh=named,
        in_specs=placed,
        out_specs=(P(), P(batch, None), P((*batch, "y"), None)),
        check_vma=False,
    )
```

```python
import functools
import math

import jax
import jax.numpy as jnp
from jax import lax
from jax.experimental import pallas as pl
from jax.experimental.pallas import tpu as pltpu
from jax.sharding import Mesh, PartitionSpec as P

X, Z, C, Y = 4, 8, 2, 4
F32, BF16 = jnp.float32, jnp.bfloat16
D = 256
IMAGES = 8
MASKED = 64
OWN_ROWS = 512
OWN_PROTOS = 128
ROWS = X * OWN_ROWS
PROTOS = Z * C * OWN_PROTOS
TOTAL_ROWS = ROWS * Z * C
PEERS = X * Y
LANES = 128
GROUPS = 16
BLOCK = 256
HALVES = BLOCK // LANES
T_SCALE = 1.0 / 0.07
S_SCALE = 1.0 / 0.1
MIB = 1 << 20
UNROLL = 8
LOG2E = math.log2(math.e)
GRAD_SCALE = 1.0 / (0.1 * TOTAL_ROWS)
VMEM_SPEC = pl.BlockSpec(memory_space=pltpu.VMEM)
KERN_BLOCKS = ROWS // BLOCK
TRANS_B = (((1,), (1,)), ((), ()))


def whole(shape):
    return pl.BlockSpec(shape, lambda *_: (0,) * len(shape))


def params(mib=32):
    return pltpu.CompilerParams(vmem_limit_bytes=mib * MIB)


def in_vmem(array):
    return pltpu.with_memory_space_constraint(array, pltpu.VMEM)


def down(row):
    return jnp.transpose(jnp.broadcast_to(row, (LANES, LANES)))


def along(column_parts):
    return jnp.sum(jnp.transpose(column_parts), axis=0, keepdims=True)


def spread(ref, first, at, row):
    ref[:, pl.ds(first + at, 1), :] = jnp.broadcast_to(row[None], (ref.shape[0], 1, LANES))


def pick_kernel(index_ref, tokens_ref, out_ref):
    for image in range(IMAGES):
        at = lax.broadcasted_iota(jnp.int32, (D, MASKED), 0)
        chosen = (at == index_ref[image : image + 1, :]).astype(BF16)
        rows = lax.dot_general(
            chosen, tokens_ref[image], (((0,), (0,)), ((), ())), preferred_element_type=F32
        )
        out_ref[image * MASKED : (image + 1) * MASKED, :] = rows.astype(BF16)


def pick_rows(index, tokens):
    return pl.pallas_call(
        pick_kernel,
        out_shape=jax.ShapeDtypeStruct((OWN_ROWS, D), BF16),
        in_specs=[whole(index.shape), whole(tokens.shape)],
        out_specs=whole((OWN_ROWS, D)),
        grid=(1,),
        compiler_params=params(),
        name="pick_rows",
    )(index, tokens)


def place_rows(pieces, out_ref):
    x = lax.axis_index("x")
    for piece, by in zip(pieces, (0, 2, 1, -1)):
        at = lax.rem(x + X - by, X) * OWN_ROWS
        out_ref[pl.ds(pl.multiple_of(at, OWN_ROWS), OWN_ROWS), :] = piece[...]


def place_protos(pieces, out_ref):
    z, core = lax.axis_index("z"), lax.axis_index("c")
    sign = 1 - 2 * core
    chips = [(z, core)]
    chips += [(lax.rem(z + Z - sign * by, Z), core) for by in (1, 2, 3)]
    chips += [(lax.rem(z + Z + sign * by, Z), 1 - core) for by in (1, 2, 3)]
    far = lax.rem(z + Z // 2, Z)
    chips += [(far, core), (far, 1 - core)]
    for piece, (chip, first) in zip(pieces, chips):
        for half in range(piece.shape[0] // OWN_PROTOS):
            which = first if half == 0 else 1 - first
            at = pl.multiple_of((chip * C + which) * OWN_PROTOS, OWN_PROTOS)
            out_ref[pl.ds(at, OWN_PROTOS), :] = piece[half * OWN_PROTOS : (half + 1) * OWN_PROTOS, :]


def block_rows(block):
    return pl.ds(pl.multiple_of(block * BLOCK, BLOCK), BLOCK)


def in_pairs(multiply, work, unroll):
    multiply(0, 0)

    def step(pair, carry):
        for parity in range(2):
            block = 2 * pair + parity
            multiply(jnp.minimum(block + 1, KERN_BLOCKS - 1), 1 - parity)
            work(block, parity)
        return carry

    lax.fori_loop(0, KERN_BLOCKS // 2, step, 0, unroll=unroll)


def teacher_kernel(*refs):
    rows_in, protos_in = refs[:X], refs[X : X + 9]
    kern_ref, top_ref, tops_ref, protos_ref, rows_ref, *scores_refs = refs[X + 9 :]
    place_rows(rows_in, rows_ref)
    place_protos(protos_in, protos_ref)

    def multiply(block, parity):
        scores_refs[parity][...] = lax.dot_general(
            rows_ref[block_rows(block), :], protos_ref[...], TRANS_B, preferred_element_type=F32
        )

    def work(block, parity):
        scores_ref = scores_refs[parity]
        for half in range(HALVES):
            at = slice(half * LANES, (half + 1) * LANES)
            group_at = block * HALVES + half
            kern_at = pl.ds(pl.multiple_of(group_at * LANES, LANES), LANES)
            top = scores_ref[at, :LANES]
            for group in range(1, GROUPS):
                top = jnp.maximum(top, scores_ref[at, group * LANES : (group + 1) * LANES])
            top = jnp.max(jnp.transpose(top), axis=0, keepdims=True)
            shift = down(top)
            for group in range(GROUPS):
                lanes = slice(group * LANES, (group + 1) * LANES)
                value = jnp.exp2((scores_ref[at, lanes] - shift) * (T_SCALE * LOG2E))
                kern_ref[kern_at, lanes] = value.astype(BF16)
            row = top * T_SCALE
            top_ref[pl.ds(group_at, 1), :] = row
            spread(tops_ref, 0, group_at, row)

    in_pairs(multiply, work, 2)


def teacher_scores(rows, protos):
    return pl.pallas_call(
        teacher_kernel,
        out_shape=(
            pltpu.VMEM((ROWS, PROTOS), BF16),
            jax.ShapeDtypeStruct((GROUPS, LANES), F32),
            jax.ShapeDtypeStruct((PEERS, GROUPS, LANES), F32),
            jax.ShapeDtypeStruct((PROTOS, D), BF16),
        ),
        in_specs=[VMEM_SPEC] * (X + 9),
        out_specs=(VMEM_SPEC,) * 4,
        scratch_shapes=[pltpu.VMEM((ROWS, D), BF16)] + [pltpu.VMEM((BLOCK, PROTOS), F32)] * 2,
        compiler_params=params(),
        name="teacher_scores",
    )(*rows, *protos)


def weight_kernel(top_ref, got_ref, out_ref):
    got = got_ref[0]
    for peer in range(1, PEERS):
        got = jnp.maximum(got, got_ref[peer])
    out_ref[...] = jnp.exp(top_ref[...] - got)


def row_weight(top, got):
    return pl.pallas_call(
        weight_kernel,
        out_shape=jax.ShapeDtypeStruct((GROUPS, LANES), F32),
        in_specs=[VMEM_SPEC] * 2,
        out_specs=VMEM_SPEC,
        compiler_params=params(),
        name="row_weight",
    )(top, got)


def column_kernel(first, weight_ref, *refs):
    if first:
        kern_ref, sums_ref, acc_ref = refs
        scaled_ref = weight_ref
    else:
        got_ref, kern_ref, sums_ref, acc_ref, scaled_ref = refs
        scaled_ref[...] = weight_ref[...] / jnp.sum(got_ref[...], axis=0)
    acc_ref[...] = jnp.zeros_like(acc_ref)

    def step(block, carry):
        rows = pl.ds(pl.multiple_of(block * LANES, LANES), LANES)
        weight = down(scaled_ref[pl.ds(block, 1), :])
        for group in range(GROUPS):
            part = kern_ref[rows, group * LANES : (group + 1) * LANES].astype(F32) * weight
            acc_ref[group] += jnp.sum(part.reshape(LANES // 8, 8, LANES), axis=0)
        return carry

    lax.fori_loop(0, GROUPS, step, 0, unroll=UNROLL)
    for group in range(GROUPS):
        spread(sums_ref, 0, group, jnp.sum(acc_ref[group], axis=0, keepdims=True))


def column_pass(weight, kern, got=None):
    first = got is None
    scratch = [pltpu.VMEM((GROUPS, 8, LANES), F32)] + ([] if first else [pltpu.VMEM((GROUPS, LANES), F32)])
    inputs = (weight,) if first else (weight, got)
    return pl.pallas_call(
        functools.partial(column_kernel, first),
        out_shape=jax.ShapeDtypeStruct((Z * C, GROUPS, LANES), F32),
        in_specs=[VMEM_SPEC] * (len(inputs) + 1),
        out_specs=VMEM_SPEC,
        scratch_shapes=scratch,
        compiler_params=params(),
        name="column_pass",
    )(*inputs, in_vmem(kern))


def row_kernel(weight_ref, got_ref, kern_ref, sums_ref, scale_ref):
    scale_ref[...] = 1.0 / jnp.sum(got_ref[...], axis=0)

    def step(block, carry):
        rows = pl.ds(pl.multiple_of(block * LANES, LANES), LANES)
        weight = down(weight_ref[pl.ds(block, 1), :])
        total = jnp.zeros((LANES, LANES), F32)
        for group in range(GROUPS):
            part = kern_ref[rows, group * LANES : (group + 1) * LANES].astype(F32) * weight
            total += part * scale_ref[group : group + 1, :]
        spread(sums_ref, 0, block, along(total))
        return carry

    lax.fori_loop(0, GROUPS, step, 0, unroll=UNROLL)


def row_pass(weight, got, kern):
    return pl.pallas_call(
        row_kernel,
        out_shape=(
            jax.ShapeDtypeStruct((PEERS, GROUPS, LANES), F32),
            jax.ShapeDtypeStruct((GROUPS, LANES), F32),
        ),
        in_specs=[VMEM_SPEC] * 3,
        out_specs=(VMEM_SPEC, VMEM_SPEC),
        compiler_params=params(),
        name="row_pass",
    )(weight, got, in_vmem(kern))


def last_kernel(weight_ref, got_ref, protos_ref, *refs):
    rows_in, (kern_ref, sums_ref, scale_ref, rows_ref, *scores_refs) = refs[:X], refs[X:]
    place_rows(rows_in, rows_ref)
    scale_ref[...] = 1.0 / jnp.sum(got_ref[...], axis=0)

    def multiply(block, parity):
        scores_refs[parity][...] = lax.dot_general(
            rows_ref[block_rows(block), :], protos_ref[...], TRANS_B, preferred_element_type=F32
        )

    def work(block, parity):
        scores_ref = scores_refs[parity]
        for half in range(HALVES):
            group_at = block * HALVES + half
            weight = down(weight_ref[pl.ds(group_at, 1), :])
            total = jnp.zeros((LANES, LANES), F32)
            crossed = jnp.zeros((LANES, LANES), F32)
            top = jnp.full((LANES, LANES), -jnp.inf, F32)
            at = slice(half * LANES, (half + 1) * LANES)
            kern_at = pl.ds(pl.multiple_of(group_at * LANES, LANES), LANES)
            for group in range(GROUPS):
                lanes = slice(group * LANES, (group + 1) * LANES)
                part = (kern_ref[kern_at, lanes].astype(F32) * weight) * scale_ref[group : group + 1, :]
                total += part
                scores = scores_ref[at, lanes]
                crossed += part * scores
                top = jnp.maximum(top, scores)
            top = jnp.max(jnp.transpose(top), axis=0, keepdims=True) * (S_SCALE * LOG2E)
            shift = down(top)
            spent = jnp.zeros((LANES, LANES), F32)
            for group in range(GROUPS):
                lanes = slice(group * LANES, (group + 1) * LANES)
                spent += jnp.exp2(scores_ref[at, lanes] * (S_SCALE * LOG2E) - shift)
            spread(sums_ref, 0, group_at, along(total))
            spread(sums_ref, GROUPS, group_at, along(crossed) * S_SCALE)
            spread(sums_ref, 2 * GROUPS, group_at, jnp.log2(along(spent)) + top)

    in_pairs(multiply, work, 1)


def last_pass(weight, got, protos, rows, kern):
    return pl.pallas_call(
        last_kernel,
        out_shape=(
            jax.ShapeDtypeStruct((PEERS, 3 * GROUPS, LANES), F32),
            jax.ShapeDtypeStruct((GROUPS, LANES), F32),
            jax.ShapeDtypeStruct((ROWS, D), BF16),
        ),
        in_specs=[VMEM_SPEC] * (X + 4),
        out_specs=(VMEM_SPEC,) * 3,
        scratch_shapes=[pltpu.VMEM((BLOCK, PROTOS), F32)] * 2,
        compiler_params=params(),
        name="last_pass",
    )(weight, got, protos, *rows, in_vmem(kern))


def grad_kernel(
    weight_ref, got_ref, scale_ref, kern_ref, rows_ref, protos_ref, student_ref, keep_ref, send_ref, loss_ref,
    scaled_ref, lse_ref, acc_ref, *scratch,
):
    scores_refs, logits_refs = scratch[:2], scratch[2:]
    sums = jnp.sum(got_ref[:, :GROUPS, :], axis=0)
    crossed = jnp.sum(got_ref[:, GROUPS : 2 * GROUPS, :], axis=0)
    top = got_ref[0, 2 * GROUPS :, :]
    for peer in range(1, PEERS):
        top = jnp.maximum(top, got_ref[peer, 2 * GROUPS :, :])
    total = jnp.zeros_like(top)
    for peer in range(PEERS):
        total += jnp.exp2(got_ref[peer, 2 * GROUPS :, :] - top)
    lse = top + jnp.log2(total)
    lse_ref[...] = lse - math.log2(GRAD_SCALE)
    scaled_ref[...] = weight_ref[...] / sums * GRAD_SCALE
    terms = (lse * math.log(2.0) * sums - crossed) / sums
    terms = jnp.sum(jnp.sum(terms, axis=0, keepdims=True), axis=1, keepdims=True)
    loss_ref[...] = jnp.broadcast_to(terms, (8, LANES))

    logits_refs[1][...] = jnp.zeros((BLOCK, PROTOS), BF16)
    acc_ref[...] = jnp.zeros_like(acc_ref)

    def multiply(block, parity):
        scores_refs[parity][...] = lax.dot_general(
            rows_ref[block_rows(block), :], protos_ref[...], TRANS_B, preferred_element_type=F32
        )

    def reduce(block, parity):
        logits = logits_refs[parity][...]
        student_ref[block_rows(block), :] = jnp.dot(
            logits, protos_ref[...], preferred_element_type=F32
        ).astype(BF16)
        acc_ref[...] += jnp.dot(
            jnp.transpose(rows_ref[block_rows(block), :]), logits, preferred_element_type=F32
        )

    def work(block, parity):
        reduce(jnp.maximum(block - 1, 0), 1 - parity)
        for half in range(HALVES):
            group_at = block * HALVES + half
            weight = down(scaled_ref[pl.ds(group_at, 1), :])
            lse = down(lse_ref[pl.ds(group_at, 1), :])
            kern_at = pl.ds(pl.multiple_of(group_at * LANES, LANES), LANES)
            for group in range(GROUPS):
                lanes = slice(group * LANES, (group + 1) * LANES)
                at = (slice(half * LANES, (half + 1) * LANES), lanes)
                target = (kern_ref[kern_at, lanes].astype(F32) * weight) * scale_ref[group : group + 1, :]
                prob = jnp.exp2(scores_refs[parity][at] * (S_SCALE * LOG2E) - lse)
                logits_refs[parity][at] = (prob - target).astype(BF16)

    in_pairs(multiply, work, 2)
    reduce(KERN_BLOCKS - 1, 1)

    core = lax.axis_index("c")
    for z in range(Z):
        for c in range(C):
            first = (z * C + c) * OWN_PROTOS
            part = jnp.transpose(acc_ref[:, first : first + OWN_PROTOS])

            @pl.when(core == c)
            def _(part=part, z=z):
                keep_ref[z] = part

            @pl.when(core != c)
            def _(part=part, z=z):
                send_ref[z] = part.astype(BF16)


def gradients(weight, got, scale, kern, rows, protos):
    return pl.pallas_call(
        grad_kernel,
        out_shape=(
            pltpu.HBM((ROWS, D), BF16),
            jax.ShapeDtypeStruct((Z, OWN_PROTOS, D), F32),
            jax.ShapeDtypeStruct((Z, OWN_PROTOS, D), BF16),
            jax.ShapeDtypeStruct((8, LANES), F32),
        ),
        in_specs=[VMEM_SPEC] * 6,
        out_specs=(VMEM_SPEC,) * 4,
        scratch_shapes=[
            pltpu.VMEM((GROUPS, LANES), F32),
            pltpu.VMEM((GROUPS, LANES), F32),
            pltpu.VMEM((D, PROTOS), F32),
        ]
        + [pltpu.VMEM((BLOCK, PROTOS), F32)] * 2
        + [pltpu.VMEM((BLOCK, PROTOS), BF16)] * 2,
        compiler_params=params(),
        name="gradients",
    )(weight, got, scale, in_vmem(kern), rows, protos)


TAIL = 16


def split_kernel(keep_ref, got_ref, loss_ref, other_ref, mine_ref, *outs):
    value = jnp.broadcast_to((loss_ref[...] + other_ref[...])[0:1, :], (TAIL, LANES))
    high = value.astype(BF16)
    rest = value - high.astype(F32)
    middle = rest.astype(BF16)
    low = (rest - middle.astype(F32)).astype(BF16)
    row = lax.broadcasted_iota(jnp.int32, (TAIL, LANES), 0)
    tail = jnp.where(row == 0, high.astype(F32), jnp.where(row == 1, middle.astype(F32), low.astype(F32)))
    tail = jnp.concatenate([tail, tail], axis=1).astype(BF16)
    for shift, out in enumerate(outs):
        at = lax.rem(lax.axis_index("z") + shift, Z)
        part = keep_ref[at] + got_ref[at].astype(F32)
        if shift == 0:
            mine_ref[...] = part
        out[:OWN_PROTOS, :] = part.astype(BF16)
        out[OWN_PROTOS:, :] = tail


def split_sums(keep, got, loss, other):
    return pl.pallas_call(
        split_kernel,
        out_shape=(jax.ShapeDtypeStruct((OWN_PROTOS, D), F32),)
        + (jax.ShapeDtypeStruct((OWN_PROTOS + TAIL, D), BF16),) * Z,
        in_specs=[VMEM_SPEC] * 4,
        out_specs=(VMEM_SPEC,) * (Z + 1),
        compiler_params=params(),
        name="split_sums",
    )(keep, got, loss, other)


def join_kernel(mine_ref, *refs):
    parts, (out_ref, loss_ref, value_ref) = refs[:Z], refs[Z:]
    total = mine_ref[...]
    for shift, part in enumerate(parts):
        if shift:
            total += part[:OWN_PROTOS, :].astype(F32)
        tail = part[OWN_PROTOS:, :LANES].astype(F32)
        at = lax.rem(lax.axis_index("z") + Z - shift, Z)
        value_ref[pl.ds(at, 1), :] = tail[0:1] + (tail[1:2] + tail[2:3])
    out_ref[...] = total
    loss = value_ref[0:1, :]
    for z in range(1, Z):
        loss = loss + value_ref[z : z + 1, :]
    loss_ref[...] = jnp.broadcast_to(loss, (8, LANES)) * (1.0 / TOTAL_ROWS)


def join_sums(mine, parts):
    return pl.pallas_call(
        join_kernel,
        out_shape=(jax.ShapeDtypeStruct((OWN_PROTOS, D), F32), jax.ShapeDtypeStruct((8, LANES), F32)),
        in_specs=[VMEM_SPEC] * (Z + 1),
        out_specs=(VMEM_SPEC, VMEM_SPEC),
        scratch_shapes=[pltpu.VMEM((Z, LANES), F32)],
        compiler_params=params(),
        name="join_sums",
    )(mine, *parts)


def shift_x(value, by):
    return lax.ppermute(value, "x", [(i, (i + by) % X) for i in range(X)])


def shift_z(value, by):
    return lax.ppermute(value, "z", [(i, (i + by) % Z) for i in range(Z)])


def swap_core(value):
    return lax.ppermute(value, "c", [(0, 1), (1, 0)])


def fan_z(value, by):
    pairs = [(z * C + c, (z + (by if c == 0 else -by)) % Z * C + c) for z in range(Z) for c in range(C)]
    return lax.ppermute(value, ("z", "c"), pairs)


def over_rows(parts):
    return lax.all_to_all(parts, ("x", "y"), 0, 0, tiled=True)


def over_protos(parts):
    return lax.all_to_all(parts, ("z", "c"), 0, 0, tiled=True)


def over_y(parts):
    return lax.all_to_all(parts, "y", 0, 0, tiled=True)


def body(teacher_tokens, student_tokens, masked_index, prototypes):
    teacher_rows = pick_rows(masked_index, teacher_tokens)
    teacher_rows, prototypes = lax.optimization_barrier((teacher_rows, prototypes))
    other = swap_core(prototypes)
    far_own = shift_z(prototypes, Z // 2)
    teacher_in = [teacher_rows] + [shift_x(teacher_rows, by) for by in (2, 1, -1)]
    chip_protos = jnp.concatenate([prototypes, other], axis=0)
    near = [fan_z(chip_protos, by) for by in (1, 2, 3)]
    far_own, near[2], student_tokens = lax.optimization_barrier((far_own, near[2], student_tokens))
    student_rows = pick_rows(masked_index, student_tokens)
    student_in = [student_rows] + [shift_x(student_rows, by) for by in (2, 1, -1)]
    protos_in = [chip_protos, *near, *[swap_core(part) for part in near], far_own, swap_core(far_own)]

    kern, top, tops, protos = teacher_scores(teacher_in, protos_in)
    weight = row_weight(top, over_rows(tops))
    weight, student_in = lax.optimization_barrier((weight, student_in))
    sums = column_pass(weight, kern)
    got, _ = row_pass(weight, over_protos(sums), kern)
    sums = column_pass(weight, kern, over_rows(got))
    got, _ = row_pass(weight, over_protos(sums), kern)
    sums = column_pass(weight, kern, over_rows(got))
    got, scale, rows = last_pass(weight, over_protos(sums), protos, student_in, kern)
    student, keep, send, loss = gradients(weight, over_rows(got), scale, kern, rows, protos)

    mine, own, *sends = split_sums(keep, swap_core(send), loss, swap_core(loss))
    parts = [own] + [None] * (Z - 1)
    for by in (4, 3, 5, 2, 6, 1, 7):
        parts[by] = shift_z(sends[by - 1], by)
    student = over_rows(student.reshape(PEERS, ROWS // PEERS, D))
    student, parts[3:6] = lax.optimization_barrier((student, parts[3:6]))
    student = jnp.sum(student.astype(F32), axis=0).astype(BF16)
    student = over_y(jnp.broadcast_to(student[None], (Y,) + student.shape))
    grad_weight, loss = join_sums(mine, parts)
    return loss[0, 0], student.reshape(OWN_ROWS, D), grad_weight


def solution(mesh):
    named = Mesh(mesh.devices.reshape(X, Z, C, Y), ("x", "z", "c", "y"))
    batch = ("x", "z", "c")
    placed = (
        P(batch, None, None),
        P(batch, None, None),
        P(batch, None),
        P((*batch, "y"), None),
    )
    return jax.shard_map(
        body,
        mesh=named,
        in_specs=placed,
        out_specs=(P(), P(batch, None), P((*batch, "y"), None)),
        check_vma=False,
    )
```
